32 devices in a mesh: ctx: 4 (over z), exp: 4 (over y, x), tp: 2 (over core).
Axes of the slice: x: 2, y: 2, z: 4, core: 2. Of those that a mesh axis runs over, the one named last changes fastest.
Arguments:
- queries: bfloat16 [16, 2, 4, 8, 128], P('ctx', 'tp', None, 'exp'), may hold values from -6 to 6
- keys: bfloat16 [128, 4, 128], P('ctx'), may hold values from -6 to 6
- values: bfloat16 [128, 4, 128], P('ctx'), may hold values from -6 to 6
- out_weight: bfloat16 [1024, 4096], P('exp'), may hold values from -0.1875 to 0.1875
- norm_gain: float32 [4096], replicated, may hold values from 0.5 to 1.5
- routes: int32 [128, 8], P(('ctx', 'exp', 'tp')), may hold values from 0 to 127, as said below
- route_weight: float32 [128, 8], P(('ctx', 'exp', 'tp')), may hold values from 0.05 to 1
- w_gate: bfloat16 [4, 4096, 384], P('exp', None, 'tp'), may hold values from -0.09375 to 0.09375
- w_up: bfloat16 [4, 4096, 384], P('exp', None, 'tp'), may hold values from -0.09375 to 0.09375
- w_down: bfloat16 [4, 384, 4096], P('exp', 'tp'), may hold values from -0.21875 to 0.21875
Outputs:
- layer_out: bfloat16 [128, 4096], P(('ctx', 'exp', 'tp'))
The draws below stay inside these ranges and needn't reach their ends.
Inputs may be any that keep to these rules, and one draw needn't show every extreme that they name: `routes`: each row names 8 different experts. In each aligned block of 4 rows no expert is named by more than 2 rows, and some expert is named by exactly 2 rows.
All inputs are finite; a program needn't handle non-finite values.
Results may differ from the reference program's by a relative error of at most 0.025.
Values may be sent and summed in bfloat16 or wider, within the bound.
No kernel may reach another device: no remote copies, remote signals or barrier semaphores. Data moves between devices by JAX's collectives and lax.ppermute only.
A program may use at most 64 MiB of HBM per device.

```python
import math
import jax
import jax.numpy as jnp
from jax import lax

D = 4096
HD = 128
KVH = 4
EXPERTS = 128
TOPK = 8
HEAD_DEV = 2
FFW = 768
CAP = 2
ROWS = 4
HEADS = 8
LIVE = 2
QBLOCKS = 16
LEN = 128
N_EXP = 4
N_TP = 2


def shuffle_row(row_key):
    return jax.random.permutation(row_key, TOPK).astype(jnp.int32)


def draw_routes(key, part):
    live_pick = min(TOPK // 2 - 1, LIVE)
    dead_count = EXPERTS - LIVE
    low_live = min(max(live_pick, -(-(ROWS * live_pick) // CAP)), LIVE)
    high_live = max(low_live, min(LIVE, ROWS * live_pick - 1))
    low_dead = max(TOPK, -(-(ROWS * TOPK) // CAP))

    def one_block(block_key):
        subkeys = jax.random.split(block_key, 7)
        modulus = jax.random.randint(subkeys[0], (), low_live, high_live + 1, dtype=jnp.int32)
        offset = jax.random.randint(subkeys[1], (), 0, modulus, dtype=jnp.int32)
        live_total = jnp.minimum(ROWS * live_pick, CAP * modulus)
        row_ids = jnp.arange(ROWS, dtype=jnp.int32)[:, None]
        col_ids = jnp.arange(TOPK, dtype=jnp.int32)[None, :]
        rank = row_ids * live_pick + col_ids
        is_live = (col_ids < live_pick) & (rank < live_total)
        live_perm = jax.random.permutation(subkeys[2], LIVE).astype(jnp.int32)
        live_ids = live_perm[(offset + rank) % modulus]
        dead_flag = jnp.where(is_live, 0, 1).astype(jnp.int32).reshape(-1)
        inactive_slot_rank = (jnp.cumsum(dead_flag) - 1).astype(jnp.int32).reshape(ROWS, TOPK)
        dead_mod = jax.random.randint(subkeys[3], (), low_dead, dead_count + 1, dtype=jnp.int32)
        dead_off = jax.random.randint(subkeys[4], (), 0, dead_mod, dtype=jnp.int32)
        dead_perm = jax.random.permutation(subkeys[5], dead_count).astype(jnp.int32)
        dead_ids = LIVE + dead_perm[(dead_off + inactive_slot_rank) % dead_mod]
        chosen = jnp.where(is_live, live_ids, dead_ids).astype(jnp.int32)
        orders = jax.vmap(shuffle_row)(jax.random.split(subkeys[6], ROWS))
        return jnp.take_along_axis(chosen, orders, axis=1)
    block_keys = jax.random.split(jax.random.fold_in(key, 7301), LEN // ROWS)
    return jax.vmap(one_block)(block_keys).reshape(LEN, TOPK).astype(jnp.int32)


def block_scale(stream_key, extent, cuts, smallest, high):
    factor_of, own = 1.0, jax.random.fold_in(stream_key, 6)
    for dim, shards_of in cuts:
        heights = jnp.exp(jax.random.uniform(jax.random.fold_in(own, dim), (shards_of,), jnp.float32, smallest / len(cuts), high / len(cuts)))
        factor_of = factor_of * jnp.repeat(heights, extent[dim] // shards_of).reshape([-1 if axis == dim else 1 for axis in range(len(extent))])
    return factor_of


def bell_draw(own_key, extent, spread, most, cuts=(), kind=jnp.bfloat16):
    factor_of = block_scale(own_key, extent, cuts, -0.22, 0.18) if cuts else 1.0
    array = jax.random.normal(own_key, extent, jnp.float32) * spread * factor_of
    return jnp.minimum(jnp.maximum(array, -most), most).astype(kind)


def setup_inputs(seed: int = 0) -> dict:
    key_of = jax.random.split(jax.random.key(seed), 11)
    queries = bell_draw(key_of[0], (QBLOCKS, N_TP, ROWS, HEADS, HD), 1.0, 6.0, ((0, 4), (1, 2), (3, 4)))
    keys = bell_draw(key_of[1], (LEN, KVH, HD), 1.0, 6.0, ((0, 4),))
    values = bell_draw(key_of[2], (LEN, KVH, HD), 1.0, 6.0, ((0, 4),))
    out_weight = bell_draw(key_of[3], (HEADS * HD, D), (HEADS * HD) ** -0.5, 0.1875, ((0, 4),))
    norm_gain = jnp.clip(1.0 + 0.1 * jax.random.normal(key_of[4], (D,), jnp.float32), 0.5, 1.5)
    routes = draw_routes(jax.random.fold_in(key_of[10], 71), 0)
    route_weight = jnp.clip(jnp.exp(math.log(1.0) - 2.9957323 * jax.random.uniform(key_of[6], (LEN, TOPK), jnp.float32) ** block_scale(key_of[6], (LEN, TOPK), ((0, 32),), -0.2, 0.2)), 0.05, 1.0)
    w_gate = bell_draw(key_of[7], (N_EXP, D, FFW // 2), D ** -0.5, 0.09375, ((0, 4), (2, 2)))
    w_up = bell_draw(key_of[8], (N_EXP, D, FFW // 2), D ** -0.5, 0.09375, ((0, 4), (2, 2)))
    w_down = bell_draw(key_of[9], (N_EXP, FFW // 2, D), FFW ** -0.5, 0.21875, ((0, 4), (1, 2)))
    return {"queries": queries, "keys": keys, "values": values, "out_weight": out_weight, "norm_gain": norm_gain, "routes": routes, "route_weight": route_weight, "w_gate": w_gate, "w_up": w_up, "w_down": w_down}


def silu_mul(gate, up):
    return gate / (1.0 + jnp.exp(-gate)) * up

def block_targets(block_routes, live_count):
    flat = block_routes.reshape(-1)
    order = jnp.arange(flat.shape[0], dtype=jnp.int32)
    same = (flat[:, None] == flat[None, :]) & (order[None, :] < order[:, None])
    slot = lax.optimization_barrier(jnp.sum(same.astype(jnp.int32), axis=1))
    return jnp.where(flat < live_count, flat * CAP + slot, -1)

def reference(queries, keys, values, out_weight, norm_gain, routes, route_weight, w_gate, w_up, w_down):
    heads = HEAD_DEV * N_EXP
    group = heads // KVH
    query_all = queries.reshape(LEN, heads, HD)
    score_scale = HD ** (-0.5)
    position = jnp.arange(LEN, dtype=jnp.int32)
    allowed = position[None, :] <= position[:, None]

    def attend(head):
        query_vector = lax.dynamic_index_in_dim(query_all, head, 1, keepdims=False)
        key = lax.dynamic_index_in_dim(keys, head // group, 1, keepdims=False)
        value = lax.dynamic_index_in_dim(values, head // group, 1, keepdims=False)
        logit_score = jnp.dot(query_vector, key.T, preferred_element_type=jnp.float32) * score_scale
        logit_score = jnp.where(allowed, logit_score, -1e+30)
        highest = lax.optimization_barrier(jnp.max(logit_score, axis=1, keepdims=True))
        attention_probability = jnp.where(allowed, jnp.exp(logit_score - highest), 0.0)
        total = lax.optimization_barrier(jnp.sum(attention_probability, axis=1, keepdims=True))
        mixed = jnp.dot(attention_probability.astype(jnp.bfloat16), value, preferred_element_type=jnp.float32)
        return (mixed / total).astype(jnp.bfloat16)
    attended = lax.map(attend, jnp.arange(heads, dtype=jnp.int32))
    per_group = attended.reshape(N_EXP, HEAD_DEV, LEN, HD).transpose(0, 2, 1, 3).reshape(N_EXP, LEN, HEAD_DEV * HD)
    weight_groups = out_weight.reshape(N_EXP, HEAD_DEV * HD, D)

    def add_group(total, pair):
        group_rows, weight = pair
        term = jnp.dot(group_rows, weight, preferred_element_type=jnp.float32).astype(jnp.bfloat16)
        term = lax.optimization_barrier(term)
        return (total + term.astype(jnp.float32), None)
    summed, _ = lax.scan(add_group, jnp.zeros((LEN, D), jnp.float32), (per_group, weight_groups))
    state = summed.astype(jnp.bfloat16)
    state_wide = state.astype(jnp.float32)
    inverse = lax.rsqrt(lax.optimization_barrier(jnp.mean(state_wide * state_wide, axis=1, keepdims=True)) + 1e-06)
    normed = (state_wide * inverse * norm_gain.astype(jnp.float32)[None, :]).astype(jnp.bfloat16)
    live_count = N_EXP // 2
    blocks = LEN // ROWS
    normed_blocks = normed.reshape(blocks, ROWS, D)
    route_blocks = routes.reshape(blocks, ROWS, TOPK)
    weight_blocks = route_weight.reshape(blocks, ROWS, TOPK)

    def build(block_routes, block_rows, block_weight):
        target = block_targets(block_routes, live_count)
        slots = jnp.arange(live_count * CAP, dtype=jnp.int32)
        hit = (target[None, :] == slots[:, None]).astype(jnp.float32).reshape(live_count * CAP, ROWS, TOPK)
        pick = lax.optimization_barrier(jnp.sum(hit, axis=2)).astype(jnp.bfloat16)
        buffer = jnp.dot(pick, block_rows, preferred_element_type=jnp.float32).astype(jnp.bfloat16)
        share = block_weight / lax.optimization_barrier(jnp.sum(block_weight, axis=1, keepdims=True))
        mix = lax.optimization_barrier(jnp.sum(hit * share[None, :, :], axis=2)).T
        return (buffer.reshape(live_count, CAP, D), mix)
    buffers, mixes = jax.vmap(build)(route_blocks, normed_blocks, weight_blocks)
    part = FFW // (2 * N_TP)

    def expert(total, index):
        expert_rows = lax.dynamic_index_in_dim(buffers, index, 1, keepdims=False).reshape(blocks * CAP, D)
        result = jnp.zeros((blocks * CAP, D), jnp.float32)
        for half in range(2):
            gate_all = lax.dynamic_index_in_dim(w_gate, half * live_count + index, 0, keepdims=False)
            up_all = lax.dynamic_index_in_dim(w_up, half * live_count + index, 0, keepdims=False)
            down_all = lax.dynamic_index_in_dim(w_down, half * live_count + index, 0, keepdims=False)
            for lane in range(N_TP):
                gate = jnp.dot(expert_rows, gate_all[:, lane * part:(lane + 1) * part], preferred_element_type=jnp.float32)
                up = jnp.dot(expert_rows, up_all[:, lane * part:(lane + 1) * part], preferred_element_type=jnp.float32)
                hidden = silu_mul(gate, up).astype(jnp.bfloat16)
                piece = jnp.dot(hidden, down_all[lane * part:(lane + 1) * part, :], preferred_element_type=jnp.float32).astype(jnp.bfloat16)
                piece = lax.optimization_barrier(piece)
                result = result + piece.astype(jnp.float32)
        mix_part = lax.dynamic_slice_in_dim(mixes, index * CAP, CAP, 2)
        contrib = jnp.einsum('brc,bcd->brd', mix_part, result.reshape(blocks, CAP, D), precision=lax.Precision.HIGHEST)
        return (total + contrib, None)
    moe, _ = lax.scan(expert, jnp.zeros((blocks, ROWS, D), jnp.float32), jnp.arange(live_count, dtype=jnp.int32))
    return (state_wide + moe.reshape(LEN, D)).astype(jnp.bfloat16)
```

```python
import jax
import jax.numpy as jnp
from jax import lax
from jax.sharding import PartitionSpec as P

CAP = 2


def silu_mul(gate, up):
    return gate / (1.0 + jnp.exp(-gate)) * up


def swap(x, axis, mask):
    size = lax.axis_size(axis)
    return lax.ppermute(x, axis, [(i, i ^ mask) for i in range(size)])


def swap_by_core(x, axis, masks):
    size, cores = lax.axis_size(axis), lax.axis_size("tp")
    pairs = [
        (i * cores + t, (i ^ masks[t % len(masks)]) * cores + t)
        for i in range(size)
        for t in range(cores)
    ]
    return lax.ppermute(x, (axis, "tp"), pairs)


def gather_ctx(x):
    size = lax.axis_size("ctx")
    first = lax.axis_index("tp") == 0
    got = [(0, x)]
    for low in range(1, size // 2):
        high = size - low
        mine = swap_by_core(x, "ctx", (low, high))
        got.append((jnp.where(first, low, high), mine))
        got.append((jnp.where(first, high, low), swap(mine, "tp", 1)))
    got.append((size // 2, swap(x, "ctx", size // 2)))
    return got


def on_device(
    queries, keys, values, out_weight, norm_gain, routes, route_weight, w_gate, w_up, w_down
):
    blocks, lanes, rows, local_heads, head_dim = queries.shape
    width = out_weight.shape[1]
    n_exp = lax.axis_size("exp")
    n_tp = lax.axis_size("tp")
    live_count = n_exp // 2
    ctx_index = lax.axis_index("ctx")
    exp_index = lax.axis_index("exp")
    tp_index = lax.axis_index("tp")
    group = local_heads * n_exp // keys.shape[1]
    kv_head = exp_index * local_heads // group
    span = keys.shape[0]
    key_mine = lax.dynamic_index_in_dim(keys, kv_head, 1, keepdims=False)
    value_mine = lax.dynamic_index_in_dim(values, kv_head, 1, keepdims=False)
    query_rows = blocks * rows
    query_vector = queries.reshape(query_rows, local_heads, head_dim).transpose(1, 0, 2)
    block_ids = jnp.arange(blocks, dtype=jnp.int32)[:, None]
    inner = jnp.arange(rows, dtype=jnp.int32)[None, :]
    query_pos = (((ctx_index * blocks + block_ids) * n_tp + tp_index) * rows + inner).reshape(-1)
    score_scale = head_dim ** (-0.5)

    got = gather_ctx(jnp.concatenate([key_mine, value_mine], axis=0))
    key_portion = jnp.concatenate([b[:span] for _, b in got], axis=0)
    value_portion = jnp.concatenate([b[span:] for _, b in got], axis=0)
    key_pos = jnp.concatenate(
        [(ctx_index ^ m) * span + jnp.arange(span, dtype=jnp.int32) for m, _ in got]
    )
    logit_score = (
        jnp.einsum("qbr,zr->qbz", query_vector, key_portion, preferred_element_type=jnp.float32)
        * score_scale
    )
    allowed = (key_pos[None, :] <= query_pos[:, None])[None, :, :]
    logit_score = jnp.where(allowed, logit_score, -1e30)
    high = jnp.max(logit_score, axis=2, keepdims=True)
    prob = jnp.where(allowed, jnp.exp(logit_score - high), 0.0)
    total = jnp.sum(prob, axis=2)
    accum = jnp.einsum(
        "axt,ty->axy",
        prob.astype(jnp.bfloat16),
        value_portion,
        preferred_element_type=jnp.float32,
    )
    mixed = (accum / total[:, :, None]).astype(jnp.bfloat16)
    mixed_rows = mixed.transpose(1, 0, 2).reshape(query_rows, local_heads * head_dim)
    term = jnp.dot(mixed_rows, out_weight, preferred_element_type=jnp.float32).astype(jnp.bfloat16)

    picks = routes.shape[1]
    flat = routes.reshape(-1)
    order = jnp.arange(flat.shape[0], dtype=jnp.int32)
    same = (flat[:, None] == flat[None, :]) & (order[None, :] < order[:, None])
    slot = jnp.sum(same.astype(jnp.int32), axis=1)
    target = jnp.where(flat < live_count, flat * CAP + slot, -1)
    slots = jnp.arange(live_count * CAP, dtype=jnp.int32)
    hit = (
        (target[None, :] == slots[:, None])
        .astype(jnp.float32)
        .reshape(live_count * CAP, rows, picks)
    )
    pick = jnp.sum(hit, axis=2).astype(jnp.bfloat16)
    share = route_weight / jnp.sum(route_weight, axis=1, keepdims=True)
    mix = jnp.sum(hit * share[None, :, :], axis=2).T

    pad = -(live_count * CAP) % 128
    note = jnp.pad(pick.T, ((0, 0), (0, pad)))
    note = jnp.where(
        (jnp.arange(blocks) == exp_index)[:, None, None], note[None], 0
    ).reshape(query_rows, -1)
    summed = jnp.concatenate([term, note], axis=1)
    steps = [1 << i for i in range(n_exp.bit_length() - 1)]
    for i, step in enumerate(steps):
        other = swap_by_core(summed, "exp", (step, steps[-1 - i]))
        summed = (summed.astype(jnp.float32) + other.astype(jnp.float32)).astype(jnp.bfloat16)
    state = summed[:, :width].astype(jnp.float32)
    note = summed[:, width : width + live_count * CAP]
    inverse = lax.rsqrt(jnp.mean(state * state, axis=1, keepdims=True) + 1e-06)
    normed = (state * inverse * norm_gain[None, :]).astype(jnp.bfloat16)
    expert = lax.rem(exp_index, live_count)
    note = lax.dynamic_slice_in_dim(note, expert * CAP, CAP, 1).reshape(blocks, rows, CAP)
    buffer = jnp.einsum(
        "brc,brd->bcd", note, normed.reshape(blocks, rows, width), preferred_element_type=jnp.float32
    ).astype(jnp.bfloat16)
    buffer = buffer.reshape(blocks * CAP, width)
    other = swap(buffer, "tp", 1)
    flat_rows = jnp.concatenate([buffer, other], axis=0)
    gate = jnp.dot(flat_rows, w_gate[0], preferred_element_type=jnp.float32)
    up = jnp.dot(flat_rows, w_up[0], preferred_element_type=jnp.float32)
    hidden = silu_mul(gate, up).astype(jnp.bfloat16)
    result = jnp.dot(hidden, w_down[0], preferred_element_type=jnp.float32).astype(jnp.bfloat16)
    result = result.reshape(n_tp, blocks, CAP, width)
    result = jnp.where(tp_index == 0, result, result[::-1]).transpose(1, 0, 2, 3)
    returned = lax.all_to_all(
        result.reshape(n_exp * n_tp, CAP, width), ("exp", "tp"), split_axis=0, concat_axis=0, tiled=True
    )
    expert_output_rows = jnp.sum(
        returned.astype(jnp.float32).reshape(2, live_count, n_tp, CAP, width), axis=(0, 2)
    )
    moe = jnp.dot(
        mix,
        expert_output_rows.reshape(live_count * CAP, width),
        precision=lax.Precision.HIGHEST,
        preferred_element_type=jnp.float32,
    )
    own = lax.dynamic_slice_in_dim(state, exp_index * rows, rows, 0)
    return (own + moe).astype(jnp.bfloat16)


def solution(mesh):
    in_specs = (
        P("ctx", "tp", None, "exp", None),
        P("ctx", None, None),
        P("ctx", None, None),
        P("exp", None),
        P(),
        P(("ctx", "exp", "tp"), None),
        P(("ctx", "exp", "tp"), None),
        P("exp", None, "tp"),
        P("exp", None, "tp"),
        P("exp", "tp", None),
    )
    out_specs = P(("ctx", "exp", "tp"), None)
    return jax.shard_map(
        on_device, mesh=mesh, in_specs=in_specs, out_specs=out_specs, check_vma=False
    )
```

```python
import functools

import jax
import jax.numpy as jnp
from jax import lax
from jax.experimental import pallas as pl
from jax.experimental.pallas import tpu as pltpu
from jax.sharding import PartitionSpec as P

CAP = 2
LANES = 128
VMEM_LIMIT = 24 * 1024 * 1024


def silu_mul(gate, up):
    return gate / (1.0 + jnp.exp(-gate)) * up


def swap(x, axis, mask):
    size = lax.axis_size(axis)
    return lax.ppermute(x, axis, [(i, i ^ mask) for i in range(size)])


def swap_by_core(x, axis, masks):
    size, cores = lax.axis_size(axis), lax.axis_size("tp")
    pairs = [
        (i * cores + t, (i ^ masks[t % len(masks)]) * cores + t)
        for i in range(size)
        for t in range(cores)
    ]
    return lax.ppermute(x, (axis, "tp"), pairs)


def gather_ctx(x):
    size = lax.axis_size("ctx")
    masks, got = [(0, 0)], [x]
    for low in range(1, size // 2):
        high = size - low
        mine = swap_by_core(x, "ctx", (low, high))
        masks += [(low, high), (high, low)]
        got += [mine, swap(mine, "tp", 1)]
    masks.append((size // 2, size // 2))
    got.append(swap(x, "ctx", size // 2))
    return masks, got


def call(kernel, outs, *args, flops=0, read=0, name=None):
    outs = [jax.ShapeDtypeStruct(shape, dtype) for shape, dtype in outs]
    return pl.pallas_call(
        kernel,
        out_shape=outs,
        in_specs=[pl.BlockSpec(memory_space=pltpu.VMEM)] * len(args),
        out_specs=[pl.BlockSpec(memory_space=pltpu.VMEM)] * len(outs),
        compiler_params=pltpu.CompilerParams(vmem_limit_bytes=VMEM_LIMIT),
        cost_estimate=pl.CostEstimate(flops=flops, bytes_accessed=read, transcendentals=0),
        name=name,
    )(*args)


def route_kernel(live, routes_ref, weight_ref, note_ref, mix_ref):
    rows, picks = routes_ref.shape
    width = mix_ref.shape[1]
    routes, weight = routes_ref[...], weight_ref[...]
    lane = lax.broadcasted_iota(jnp.int32, (rows, width), 1)
    expert = jnp.where(lane < live * CAP, lane // CAP, -1)
    has = jnp.zeros((rows, width), jnp.float32)
    part = jnp.zeros((rows, width), jnp.float32)
    for k in range(picks):
        hit = routes[:, k : k + 1] == expert
        has = has + jnp.where(hit, 1.0, 0.0)
        part = part + jnp.where(hit, weight[:, k : k + 1], 0.0)
    earlier = [jnp.zeros((1, width), jnp.float32)]
    for r in range(rows - 1):
        earlier.append(earlier[-1] + has[r : r + 1])
    slot = jnp.concatenate(earlier, axis=0)
    hit = jnp.where(slot == (lane % CAP).astype(jnp.float32), has, 0.0)
    mix_ref[...] = hit * part / jnp.sum(weight, axis=1, keepdims=True)
    blocks = note_ref.shape[0] // rows
    mine = lax.axis_index("exp")
    note_ref[...] = jnp.concatenate(
        [jnp.where(mine == b, hit, 0.0) for b in range(blocks)], axis=0
    ).astype(note_ref.dtype)


def attend_kernel(masks, blocks, q_ref, weight_ref, note_ref, *refs):
    kv_refs, out_ref = refs[:-1], refs[-1]
    count, heads, head_dim = q_ref.shape
    span = kv_refs[0].shape[0] // 2
    rows = count // blocks
    width = weight_ref.shape[1]
    n_tp = lax.axis_size("tp")
    ctx, core = lax.axis_index("ctx"), lax.axis_index("tp")
    query = jnp.concatenate([q_ref[:, h, :] for h in range(heads)], axis=0)
    key = jnp.concatenate([r[:span, :] for r in kv_refs], axis=0)
    value = jnp.concatenate([r[span:, :] for r in kv_refs], axis=0)
    score = lax.dot_general(
        query, key, (((1,), (1,)), ((), ())), preferred_element_type=jnp.float32
    ) * (head_dim ** (-0.5))
    lane = lax.broadcasted_iota(jnp.int32, (1, len(kv_refs) * span), 1)
    start = jnp.zeros_like(lane)
    for j, (even, odd) in enumerate(masks):
        block = ctx ^ jnp.where(core == 0, even, odd)
        start = jnp.where(lane // span == j, block * span, start)
    key_pos = start + lane % span
    row = lax.broadcasted_iota(jnp.int32, (heads * count, 1), 0) % count
    query_pos = ((ctx * blocks + row // rows) * n_tp + core) * rows + row % rows
    allowed = key_pos <= query_pos
    score = jnp.where(allowed, score, -1e30)
    prob = jnp.where(allowed, jnp.exp(score - jnp.max(score, axis=1, keepdims=True)), 0.0)
    total = jnp.sum(prob, axis=1, keepdims=True)
    mixed = jnp.dot(prob.astype(jnp.bfloat16), value, preferred_element_type=jnp.float32) / total
    mixed = mixed.astype(jnp.bfloat16)
    mixed = jnp.concatenate([mixed[h * count : (h + 1) * count] for h in range(heads)], axis=1)
    out_ref[:, :width] = jnp.dot(
        mixed, weight_ref[...], preferred_element_type=jnp.float32
    ).astype(out_ref.dtype)
    out_ref[:, width:] = note_ref[...]


def norm_kernel(blocks, live, mine_ref, other_ref, gain_ref, state_ref, buffer_ref):
    count, width = state_ref.shape
    rows = count // blocks
    summed = (mine_ref[:, :width].astype(jnp.float32) + other_ref[:, :width].astype(jnp.float32)).astype(
        jnp.bfloat16
    )
    state_ref[...] = summed
    state = summed.astype(jnp.float32)
    note = mine_ref[:, width:] + other_ref[:, width:]
    inverse = lax.rsqrt(jnp.mean(state * state, axis=1, keepdims=True) + 1e-06)
    normed = (state * inverse * gain_ref[...]).astype(jnp.bfloat16)
    expert = lax.rem(lax.axis_index("exp"), live)
    slots = blocks * CAP
    shape = (slots, note.shape[1])
    pick_lane = (
        lax.broadcasted_iota(jnp.int32, shape, 1)
        == expert * CAP + lax.broadcasted_iota(jnp.int32, shape, 0) % CAP
    )
    pick = lax.dot_general(
        pick_lane.astype(jnp.float32).astype(jnp.bfloat16),
        note,
        (((1,), (1,)), ((), ())),
        preferred_element_type=jnp.float32,
    )
    shape = (slots, count)
    same = (
        lax.broadcasted_iota(jnp.int32, shape, 0) // CAP
        == lax.broadcasted_iota(jnp.int32, shape, 1) // rows
    )
    pick = jnp.where(same, pick, 0.0).astype(jnp.bfloat16)
    buffer_ref[...] = jnp.dot(pick, normed, preferred_element_type=jnp.float32).astype(jnp.bfloat16)


def expert_kernel(mine_ref, other_ref, gate_ref, up_ref, down_ref, out_ref):
    slots = mine_ref.shape[0]
    x = jnp.concatenate([mine_ref[...], other_ref[...]], axis=0)
    last = (((1,), (1,)), ((), ()))
    gate = lax.dot_general(x, gate_ref[...], last, preferred_element_type=jnp.float32)
    up = lax.dot_general(x, up_ref[...], last, preferred_element_type=jnp.float32)
    hidden = silu_mul(gate, up).astype(jnp.bfloat16)
    result = jnp.dot(hidden, down_ref[...], preferred_element_type=jnp.float32).astype(jnp.bfloat16)
    core = lax.axis_index("tp")
    for half in range(2):
        for b in range(slots // CAP):
            at = half * slots + b * CAP
            out_ref[2 * b + (core ^ half)] = result[at : at + CAP]


def combine_kernel(live, back_ref, mix_ref, own_ref, out_ref):
    n_tp = lax.axis_size("tp")
    mix = mix_ref[...]
    total = own_ref[...].astype(jnp.float32)
    for x in range(live):
        parts = [back_ref[(h * live + x) * n_tp + t] for h in range(2) for t in range(n_tp)]
        rows = functools.reduce(lambda a, b: a + b, [p.astype(jnp.float32) for p in parts])
        for s in range(CAP):
            lane = x * CAP + s
            total = total + mix[:, lane : lane + 1] * rows[s : s + 1]
    out_ref[...] = total.astype(out_ref.dtype)


def on_device(
    queries, keys, values, out_weight, norm_gain, routes, route_weight, w_gate, w_up, w_down
):
    blocks, lanes, rows, local_heads, head_dim = queries.shape
    width = out_weight.shape[1]
    n_exp = lax.axis_size("exp")
    n_tp = lax.axis_size("tp")
    live = n_exp // 2
    count = blocks * rows
    exp_index = lax.axis_index("exp")
    group = local_heads * n_exp // keys.shape[1]
    kv_head = exp_index * local_heads // group
    key_mine = lax.dynamic_index_in_dim(keys, kv_head, 1, keepdims=False)
    value_mine = lax.dynamic_index_in_dim(values, kv_head, 1, keepdims=False)
    masks, got = gather_ctx(jnp.concatenate([key_mine, value_mine], axis=0))

    note_width = -(-(live * CAP) // LANES) * LANES
    note, mix = call(
        functools.partial(route_kernel, live),
        [((count, note_width), jnp.bfloat16), ((rows, note_width), jnp.float32)],
        routes,
        route_weight,
        name="route",
    )
    (summed,) = call(
        functools.partial(attend_kernel, masks, blocks),
        [((count, width + note_width), jnp.bfloat16)],
        queries.reshape(count, local_heads, head_dim),
        out_weight,
        note,
        *got,
        flops=2 * count * out_weight.size,
        read=2 * out_weight.size,
        name="attend",
    )
    steps = [1 << i for i in range(n_exp.bit_length() - 1)]
    for i, step in enumerate(steps):
        other = swap_by_core(summed, "exp", (step, steps[-1 - i]))
        if i < len(steps) - 1:
            summed = (summed.astype(jnp.float32) + other.astype(jnp.float32)).astype(jnp.bfloat16)
    state, buffer = call(
        functools.partial(norm_kernel, blocks, live),
        [((count, width), jnp.bfloat16), ((blocks * CAP, width), jnp.bfloat16)],
        summed,
        other,
        norm_gain.reshape(1, width),
        name="norm",
    )
    (result,) = call(
        expert_kernel,
        [((n_exp * n_tp, CAP, width), jnp.bfloat16)],
        buffer,
        swap(buffer, "tp", 1),
        w_gate[0].T,
        w_up[0].T,
        w_down[0],
        flops=2 * blocks * CAP * n_tp * 3 * w_down.size,
        read=6 * w_down.size,
        name="experts",
    )
    back = lax.all_to_all(result, ("exp", "tp"), split_axis=0, concat_axis=0, tiled=True)
    own = lax.dynamic_slice_in_dim(state, exp_index * rows, rows, 0)
    (out,) = call(
        functools.partial(combine_kernel, live),
        [((rows, width), jnp.bfloat16)],
        back,
        mix,
        own,
        name="combine",
    )
    return out


def solution(mesh):
    in_specs = (
        P("ctx", "tp", None, "exp", None),
        P("ctx", None, None),
        P("ctx", None, None),
        P("exp", None),
        P(),
        P(("ctx", "exp", "tp"), None),
        P(("ctx", "exp", "tp"), None),
        P("exp", None, "tp"),
        P("exp", None, "tp"),
        P("exp", "tp", None),
    )
    out_specs = P(("ctx", "exp", "tp"), None)
    return jax.shard_map(
        on_device, mesh=mesh, in_specs=in_specs, out_specs=out_specs, check_vma=False
    )
```

```python
import functools

import jax
import jax.numpy as jnp
from jax import lax
from jax.experimental import pallas as pl
from jax.experimental.pallas import tpu as pltpu
from jax.sharding import PartitionSpec as P

CAP = 2
LANES = 128
VMEM_LIMIT = 24 * 1024 * 1024


def silu_mul(gate, up):
    return gate / (1.0 + jnp.exp(-gate)) * up


def swap(x, axis, mask):
    size = lax.axis_size(axis)
    return lax.ppermute(x, axis, [(i, i ^ mask) for i in range(size)])


def swap_by_core(x, axis, masks):
    size, cores = lax.axis_size(axis), lax.axis_size("tp")
    pairs = [
        (i * cores + t, (i ^ masks[t % len(masks)]) * cores + t)
        for i in range(size)
        for t in range(cores)
    ]
    return lax.ppermute(x, (axis, "tp"), pairs)


def gather_ctx(x):
    size = lax.axis_size("ctx")
    masks, got = [(0, 0)], [x]
    for low in range(1, size // 2):
        high = size - low
        mine = swap_by_core(x, "ctx", (low, high))
        masks += [(low, high), (high, low)]
        got += [mine, swap(mine, "tp", 1)]
    masks.append((size // 2, size // 2))
    got.append(swap(x, "ctx", size // 2))
    return masks, got


def far(args):
    return [pltpu.with_memory_space_constraint(a, pltpu.HBM) for a in args]


def call(kernel, outs, *args, where=pltpu.VMEM, scratch=(), kept=pltpu.VMEM, flops=0, read=0, name=None):
    return pl.pallas_call(
        kernel,
        out_shape=[kept(shape, dtype) for shape, dtype in outs],
        in_specs=[pl.BlockSpec(memory_space=where)] * len(args),
        out_specs=[pl.BlockSpec(memory_space=pltpu.VMEM)] * len(outs),
        scratch_shapes=scratch,
        compiler_params=pltpu.CompilerParams(vmem_limit_bytes=VMEM_LIMIT),
        cost_estimate=pl.CostEstimate(flops=flops, bytes_accessed=read, transcendentals=0),
        name=name,
    )(*args)


def open_kernel(live, blocks, group, *refs):
    ins, (kv_ref, q_ref, note_ref, mix_ref), held = refs[:5], refs[5:9], refs[9:14]
    sems = refs[14]
    copies = [pltpu.make_async_copy(i, h, sems.at[n]) for n, (i, h) in enumerate(zip(ins, held))]
    for copy in copies:
        copy.start()
    key_ref, value_ref, query_ref, routes_ref, weight_ref = held
    span = key_ref.shape[0]
    heads = query_ref.shape[1]
    mine = lax.axis_index("exp")
    kv_head = mine * heads // group
    for n, ref in enumerate((key_ref, value_ref)):
        copies[n].wait()
        wanted = lax.broadcasted_iota(jnp.int32, ref.shape, 1) == kv_head
        kept = jnp.sum(jnp.where(wanted, ref[...].astype(jnp.float32), 0.0), axis=1)
        kv_ref[n * span : (n + 1) * span, :] = kept.astype(kv_ref.dtype)
    copies[2].wait()
    q_ref[...] = jnp.concatenate([query_ref[:, h, :] for h in range(heads)], axis=0)
    copies[3].wait()
    copies[4].wait()
    rows, picks = routes_ref.shape
    width = mix_ref.shape[1]
    routes, weight = routes_ref[...], weight_ref[...]
    lane = lax.broadcasted_iota(jnp.int32, (rows, width), 1)
    expert = jnp.where(lane < live * CAP, lane // CAP, -1)
    has = jnp.zeros((rows, width), jnp.float32)
    part = jnp.zeros((rows, width), jnp.float32)
    for k in range(picks):
        hit = routes[:, k : k + 1] == expert
        has = has + jnp.where(hit, 1.0, 0.0)
        part = part + jnp.where(hit, weight[:, k : k + 1], 0.0)
    earlier = [jnp.zeros((1, width), jnp.float32)]
    for r in range(rows - 1):
        earlier.append(earlier[-1] + has[r : r + 1])
    slot = jnp.concatenate(earlier, axis=0)
    hit = jnp.where(slot == (lane % CAP).astype(jnp.float32), has, 0.0)
    mix_ref[...] = hit * part / jnp.sum(weight, axis=1, keepdims=True)
    note_ref[...] = jnp.concatenate(
        [jnp.where(mine == b, hit, 0.0) for b in range(blocks)], axis=0
    ).astype(note_ref.dtype)


def attend_kernel(masks, blocks, q_ref, *refs):
    kv_refs, out_ref = refs[:-1], refs[-1]
    count = out_ref.shape[0]
    heads = q_ref.shape[0] // count
    head_dim = q_ref.shape[1]
    span = kv_refs[0].shape[0] // 2
    rows = count // blocks
    n_tp = lax.axis_size("tp")
    ctx, core = lax.axis_index("ctx"), lax.axis_index("tp")
    key = jnp.concatenate([r[:span, :] for r in kv_refs], axis=0)
    value = jnp.concatenate([r[span:, :] for r in kv_refs], axis=0)
    score = lax.dot_general(
        q_ref[...], key, (((1,), (1,)), ((), ())), preferred_element_type=jnp.float32
    ) * (head_dim ** (-0.5))
    lane = lax.broadcasted_iota(jnp.int32, (1, len(kv_refs) * span), 1)
    start = jnp.zeros_like(lane)
    for j, (even, odd) in enumerate(masks):
        block = ctx ^ jnp.where(core == 0, even, odd)
        start = jnp.where(lane // span == j, block * span, start)
    key_pos = start + lane % span
    row = lax.broadcasted_iota(jnp.int32, (heads * count, 1), 0) % count
    query_pos = ((ctx * blocks + row // rows) * n_tp + core) * rows + row % rows
    allowed = key_pos <= query_pos
    score = jnp.where(allowed, score, -1e30)
    prob = jnp.where(allowed, jnp.exp(score - jnp.max(score, axis=1, keepdims=True)), 0.0)
    total = jnp.sum(prob, axis=1, keepdims=True)
    mixed = jnp.dot(prob.astype(jnp.bfloat16), value, preferred_element_type=jnp.float32) / total
    mixed = mixed.astype(jnp.bfloat16)
    for h in range(heads):
        out_ref[:, h * head_dim : (h + 1) * head_dim] = mixed[h * count : (h + 1) * count]


def load_kernel(*refs):
    n = len(refs) // 2
    copies = [pltpu.make_async_copy(refs[i], refs[n + i], refs[-1].at[i]) for i in range(n)]
    for copy in copies:
        copy.start()
    for copy in copies:
        copy.wait()


def load(weights, name):
    return call(
        load_kernel,
        [(w.shape, w.dtype) for w in weights],
        *far(weights),
        where=pltpu.HBM,
        scratch=[pltpu.SemaphoreType.DMA((len(weights),))],
        read=2 * sum(w.size for w in weights),
        name=name,
    )


def hidden_units(x, gate_ref, up_ref, down_ref):
    last = (((1,), (1,)), ((), ()))
    gate = lax.dot_general(x, gate_ref[...], last, preferred_element_type=jnp.float32)
    up = lax.dot_general(x, up_ref[...], last, preferred_element_type=jnp.float32)
    hidden = silu_mul(gate, up).astype(jnp.bfloat16)
    return jnp.dot(hidden, down_ref[...], preferred_element_type=jnp.float32)


def first_kernel(blocks, live, mine_ref, other_ref, gain_ref, gate_ref, up_ref, down_ref, *outs):
    own_ref, x_ref, part_ref = outs
    count, width = mine_ref.shape[0], x_ref.shape[1]
    rows = count // blocks
    mine = lax.axis_index("exp")
    summed = (mine_ref[:, :width].astype(jnp.float32) + other_ref[:, :width].astype(jnp.float32)).astype(
        jnp.bfloat16
    )
    shape = (rows, count)
    own = (
        lax.broadcasted_iota(jnp.int32, shape, 0) + mine * rows
        == lax.broadcasted_iota(jnp.int32, shape, 1)
    )
    own = own.astype(jnp.float32).astype(jnp.bfloat16)
    own_ref[...] = jnp.dot(own, summed, preferred_element_type=jnp.float32)
    state = summed.astype(jnp.float32)
    note = mine_ref[:, width:] + other_ref[:, width:]
    inverse = lax.rsqrt(jnp.mean(state * state, axis=1, keepdims=True) + 1e-06)
    normed = (state * inverse * gain_ref[...]).astype(jnp.bfloat16)
    expert = lax.rem(mine, live)
    slots = blocks * CAP
    shape = (slots, note.shape[1])
    pick_lane = (
        lax.broadcasted_iota(jnp.int32, shape, 1)
        == expert * CAP + lax.broadcasted_iota(jnp.int32, shape, 0) % CAP
    )
    pick = lax.dot_general(
        pick_lane.astype(jnp.float32).astype(jnp.bfloat16),
        note,
        (((1,), (1,)), ((), ())),
        preferred_element_type=jnp.float32,
    )
    shape = (slots, count)
    same = (
        lax.broadcasted_iota(jnp.int32, shape, 0) // CAP
        == (lax.broadcasted_iota(jnp.int32, shape, 1) // rows) ^ mine
    )
    pick = jnp.where(same, pick, 0.0).astype(jnp.bfloat16)
    x = jnp.dot(pick, normed, preferred_element_type=jnp.float32).astype(jnp.bfloat16)
    x_ref[...] = x
    part_ref[...] = hidden_units(x, gate_ref, up_ref, down_ref)


def second_kernel(x_ref, part_ref, gate_ref, up_ref, down_ref, *outs):
    result = part_ref[...] + hidden_units(x_ref[...], gate_ref, up_ref, down_ref)
    for m, out_ref in enumerate(outs):
        out_ref[...] = result[m * CAP : (m + 1) * CAP].astype(out_ref.dtype)


def combine_kernel(live, mix_ref, own_ref, *refs):
    back_refs, out_ref = refs[:-1], refs[-1]
    mine = lax.axis_index("exp")
    mix = mix_ref[...]
    lane = lax.broadcasted_iota(jnp.int32, mix.shape, 1)
    total = own_ref[...]
    for m, back_ref in enumerate(back_refs):
        expert = lax.rem(mine ^ m, live)
        back = back_ref[...].astype(jnp.float32)
        for s in range(CAP):
            share = jnp.sum(jnp.where(lane == expert * CAP + s, mix, 0.0), axis=1, keepdims=True)
            total = total + share * back[s : s + 1]
    out_ref[...] = total.astype(out_ref.dtype)


def on_device(
    queries, keys, values, out_weight, norm_gain, routes, route_weight, w_gate, w_up, w_down
):
    blocks, lanes, rows, heads, head_dim = queries.shape
    width = out_weight.shape[1]
    n_exp = lax.axis_size("exp")
    live = n_exp // 2
    count = blocks * rows
    group = heads * n_exp // keys.shape[1]
    note_width = -(-(live * CAP) // LANES) * LANES
    small = (keys, values, queries.reshape(count, heads, head_dim), routes, route_weight)
    kv, query, note, mix = call(
        functools.partial(open_kernel, live, blocks, group),
        [
            ((2 * keys.shape[0], head_dim), jnp.bfloat16),
            ((heads * count, head_dim), jnp.bfloat16),
            ((count, note_width), jnp.bfloat16),
            ((rows, note_width), jnp.float32),
        ],
        *far(small),
        where=pltpu.HBM,
        scratch=[pltpu.VMEM(a.shape, a.dtype) for a in small] + [pltpu.SemaphoreType.DMA((5,))],
        name="open",
    )
    masks, got = gather_ctx(kv)
    (mixed,) = call(
        functools.partial(attend_kernel, masks, blocks),
        [((count, heads * head_dim), jnp.bfloat16)],
        query,
        *got,
        name="attend",
    )
    term = jnp.dot(mixed, out_weight, preferred_element_type=jnp.float32).astype(jnp.bfloat16)
    summed = jnp.concatenate([term, note], axis=1)
    weights = (w_gate[0].T, w_up[0].T, w_down[0])
    got[1], *moving = lax.optimization_barrier((got[1], *weights))
    moved = [swap(w, "tp", 1) for w in moving]
    summed, *weights = lax.optimization_barrier((summed, *weights))
    weights = load(weights, "load_mine")
    steps = [1 << i for i in range(n_exp.bit_length() - 1)]
    for i, step in enumerate(steps):
        other = swap_by_core(summed, "exp", (step, steps[-1 - i]))
        if i < len(steps) - 1:
            summed = (summed.astype(jnp.float32) + other.astype(jnp.float32)).astype(jnp.bfloat16)
    slots = blocks * CAP
    own, x, part = call(
        functools.partial(first_kernel, blocks, live),
        [
            ((rows, width), jnp.float32),
            ((slots, width), jnp.bfloat16),
            ((slots, width), jnp.float32),
        ],
        summed,
        other,
        norm_gain.reshape(1, width),
        *weights,
        flops=6 * slots * w_down.size,
        read=6 * w_down.size,
        name="first",
    )
    results = call(
        second_kernel,
        [((CAP, width), jnp.bfloat16)] * n_exp,
        x,
        part,
        *moved,
        flops=6 * slots * w_down.size,
        read=6 * w_down.size,
        name="second",
    )
    back = [results[0]] + [swap(r, "exp", m) for m, r in enumerate(results) if m]
    (out,) = call(
        functools.partial(combine_kernel, live),
        [((rows, width), jnp.bfloat16)],
        mix,
        own,
        *back,
        kept=jax.ShapeDtypeStruct,
        name="combine",
    )
    return out


def solution(mesh):
    in_specs = (
        P("ctx", "tp", None, "exp", None),
        P("ctx", None, None),
        P("ctx", None, None),
        P("exp", None),
        P(),
        P(("ctx", "exp", "tp"), None),
        P(("ctx", "exp", "tp"), None),
        P("exp", None, "tp"),
        P("exp", None, "tp"),
        P("exp", "tp", None),
    )
    out_specs = P(("ctx", "exp", "tp"), None)
    return jax.shard_map(
        on_device, mesh=mesh, in_specs=in_specs, out_specs=out_specs, check_vma=False
    )
```

```python
import functools

import jax
import jax.numpy as jnp
from jax import lax
from jax.experimental import pallas as pl
from jax.experimental.pallas import tpu as pltpu
from jax.sharding import PartitionSpec as P

CAP = 2
LANES = 128
VMEM_LIMIT = 24 * 1024 * 1024


def silu_mul(gate, up):
    return gate / (1.0 + jnp.exp(-gate)) * up


def swap(x, axis, mask):
    size = lax.axis_size(axis)
    return lax.ppermute(x, axis, [(i, i ^ mask) for i in range(size)])


def swap_by_core(x, axis, masks):
    size, cores = lax.axis_size(axis), lax.axis_size("tp")
    pairs = [
        (i * cores + t, (i ^ masks[t % len(masks)]) * cores + t)
        for i in range(size)
        for t in range(cores)
    ]
    return lax.ppermute(x, (axis, "tp"), pairs)


def gather_ctx(x):
    size = lax.axis_size("ctx")
    masks, got = [(0, 0)], [x]
    for low in range(1, size // 2):
        high = size - low
        mine = swap_by_core(x, "ctx", (low, high))
        masks += [(low, high), (high, low)]
        got += [mine, swap(mine, "tp", 1)]
    masks.append((size // 2, size // 2))
    got.append(swap(x, "ctx", size // 2))
    return masks, got


def far(args):
    return [pltpu.with_memory_space_constraint(a, pltpu.HBM) for a in args]


def call(kernel, outs, *args, where=pltpu.VMEM, scratch=(), kept=pltpu.VMEM, flops=0, read=0, name=None):
    return pl.pallas_call(
        kernel,
        out_shape=[kept(shape, dtype) for shape, dtype in outs],
        in_specs=[pl.BlockSpec(memory_space=where)] * len(args),
        out_specs=[pl.BlockSpec(memory_space=pltpu.VMEM)] * len(outs),
        scratch_shapes=scratch,
        compiler_params=pltpu.CompilerParams(vmem_limit_bytes=VMEM_LIMIT),
        cost_estimate=pl.CostEstimate(flops=flops, bytes_accessed=read, transcendentals=0),
        name=name,
    )(*args)


def open_kernel(heads, group, key_hbm, value_hbm, kv_ref, key_ref, value_ref, sems):
    copies = [
        pltpu.make_async_copy(key_hbm, key_ref, sems.at[0]),
        pltpu.make_async_copy(value_hbm, value_ref, sems.at[1]),
    ]
    for copy in copies:
        copy.start()
    span = key_ref.shape[0]
    kv_head = lax.axis_index("exp") * heads // group
    for n, ref in enumerate((key_ref, value_ref)):
        copies[n].wait()
        wanted = lax.broadcasted_iota(jnp.int32, ref.shape, 1) == kv_head
        kept = jnp.sum(jnp.where(wanted, ref[...].astype(jnp.float32), 0.0), axis=1)
        kv_ref[n * span : (n + 1) * span, :] = kept.astype(kv_ref.dtype)


def route_kernel(live, blocks, *refs):
    ins, (q_ref, note_ref, mix_ref), held, sems = refs[:3], refs[3:6], refs[6:9], refs[9]
    copies = [pltpu.make_async_copy(i, h, sems.at[n]) for n, (i, h) in enumerate(zip(ins, held))]
    for copy in copies:
        copy.start()
    query_ref, routes_ref, weight_ref = held
    heads = query_ref.shape[1]
    mine = lax.axis_index("exp")
    for copy in copies:
        copy.wait()
    q_ref[...] = jnp.concatenate([query_ref[:, h, :] for h in range(heads)], axis=0)
    rows, picks = routes_ref.shape
    width = mix_ref.shape[1]
    routes, weight = routes_ref[...], weight_ref[...]
    lane = lax.broadcasted_iota(jnp.int32, (rows, width), 1)
    expert = jnp.where(lane < live * CAP, lane // CAP, -1)
    has = jnp.zeros((rows, width), jnp.float32)
    part = jnp.zeros((rows, width), jnp.float32)
    for k in range(picks):
        hit = routes[:, k : k + 1] == expert
        has = has + jnp.where(hit, 1.0, 0.0)
        part = part + jnp.where(hit, weight[:, k : k + 1], 0.0)
    earlier = [jnp.zeros((1, width), jnp.float32)]
    for r in range(rows - 1):
        earlier.append(earlier[-1] + has[r : r + 1])
    slot = jnp.concatenate(earlier, axis=0)
    hit = jnp.where(slot == (lane % CAP).astype(jnp.float32), has, 0.0)
    mix_ref[...] = hit * part / jnp.sum(weight, axis=1, keepdims=True)
    note_ref[...] = jnp.concatenate(
        [jnp.where(mine == b, hit, 0.0) for b in range(blocks)], axis=0
    ).astype(note_ref.dtype)


def attend_kernel(masks, blocks, q_ref, *refs):
    kv_refs, out_ref = refs[:-1], refs[-1]
    count = out_ref.shape[0]
    heads = q_ref.shape[0] // count
    head_dim = q_ref.shape[1]
    span = kv_refs[0].shape[0] // 2
    rows = count // blocks
    n_tp = lax.axis_size("tp")
    ctx, core = lax.axis_index("ctx"), lax.axis_index("tp")
    key = jnp.concatenate([r[:span, :] for r in kv_refs], axis=0)
    value = jnp.concatenate([r[span:, :] for r in kv_refs], axis=0)
    score = lax.dot_general(
        q_ref[...], key, (((1,), (1,)), ((), ())), preferred_element_type=jnp.float32
    ) * (head_dim ** (-0.5))
    lane = lax.broadcasted_iota(jnp.int32, (1, len(kv_refs) * span), 1)
    start = jnp.zeros_like(lane)
    for j, (even, odd) in enumerate(masks):
        block = ctx ^ jnp.where(core == 0, even, odd)
        start = jnp.where(lane // span == j, block * span, start)
    key_pos = start + lane % span
    row = lax.broadcasted_iota(jnp.int32, (heads * count, 1), 0) % count
    query_pos = ((ctx * blocks + row // rows) * n_tp + core) * rows + row % rows
    allowed = key_pos <= query_pos
    score = jnp.where(allowed, score, -1e30)
    prob = jnp.where(allowed, jnp.exp(score - jnp.max(score, axis=1, keepdims=True)), 0.0)
    total = jnp.sum(prob, axis=1, keepdims=True)
    mixed = jnp.dot(prob.astype(jnp.bfloat16), value, preferred_element_type=jnp.float32) / total
    mixed = mixed.astype(jnp.bfloat16)
    for h in range(heads):
        out_ref[:, h * head_dim : (h + 1) * head_dim] = mixed[h * count : (h + 1) * count]


def load_kernel(*refs):
    n = len(refs) // 2
    copies = [pltpu.make_async_copy(refs[i], refs[n + i], refs[-1].at[i]) for i in range(n)]
    for copy in copies:
        copy.start()
    for copy in copies:
        copy.wait()


def load(weights, name):
    return call(
        load_kernel,
        [(w.shape, w.dtype) for w in weights],
        *far(weights),
        where=pltpu.HBM,
        scratch=[pltpu.SemaphoreType.DMA((len(weights),))],
        read=2 * sum(w.size for w in weights),
        name=name,
    )


def hidden_units(x, gate_ref, up_ref, down_ref):
    last = (((1,), (1,)), ((), ()))
    gate = lax.dot_general(x, gate_ref[...], last, preferred_element_type=jnp.float32)
    up = lax.dot_general(x, up_ref[...], last, preferred_element_type=jnp.float32)
    hidden = silu_mul(gate, up).astype(jnp.bfloat16)
    return jnp.dot(hidden, down_ref[...], preferred_element_type=jnp.float32)


def first_kernel(blocks, live, masks, mine_ref, other_ref, gain_ref, gate_ref, up_ref, down_ref, *outs):
    own_ref, x_ref, part_ref = outs
    count, width = mine_ref.shape[0], x_ref.shape[1]
    rows = count // blocks
    mine = lax.axis_index("exp")
    summed = (mine_ref[:, :width].astype(jnp.float32) + other_ref[:, :width].astype(jnp.float32)).astype(
        jnp.bfloat16
    )
    shape = (rows, count)
    own = (
        lax.broadcasted_iota(jnp.int32, shape, 0) + mine * rows
        == lax.broadcasted_iota(jnp.int32, shape, 1)
    )
    own = own.astype(jnp.float32).astype(jnp.bfloat16)
    own_ref[...] = jnp.dot(own, summed, preferred_element_type=jnp.float32)
    state = summed.astype(jnp.float32)
    note = mine_ref[:, width:] + other_ref[:, width:]
    inverse = lax.rsqrt(jnp.mean(state * state, axis=1, keepdims=True) + 1e-06)
    normed = (state * inverse * gain_ref[...]).astype(jnp.bfloat16)
    expert = lax.rem(mine, live)
    slots = blocks * CAP
    shape = (slots, note.shape[1])
    pick_lane = (
        lax.broadcasted_iota(jnp.int32, shape, 1)
        == expert * CAP + lax.broadcasted_iota(jnp.int32, shape, 0) % CAP
    )
    pick = lax.dot_general(
        pick_lane.astype(jnp.float32).astype(jnp.bfloat16),
        note,
        (((1,), (1,)), ((), ())),
        preferred_element_type=jnp.float32,
    )
    shape = (slots, count)
    place = lax.broadcasted_iota(jnp.int32, shape, 0) // CAP
    core = lax.axis_index("tp")
    mask = jnp.zeros(shape, jnp.int32)
    for i, (even, odd) in enumerate(masks):
        mask = jnp.where(place == i, jnp.where(core == 0, even, odd), mask)
    same = mask == (lax.broadcasted_iota(jnp.int32, shape, 1) // rows) ^ mine
    pick = jnp.where(same, pick, 0.0).astype(jnp.bfloat16)
    x = jnp.dot(pick, normed, preferred_element_type=jnp.float32).astype(jnp.bfloat16)
    x_ref[...] = x
    part_ref[...] = hidden_units(x, gate_ref, up_ref, down_ref)


def second_kernel(x_ref, part_ref, gate_ref, up_ref, down_ref, *outs):
    result = part_ref[...] + hidden_units(x_ref[...], gate_ref, up_ref, down_ref)
    for m, out_ref in enumerate(outs):
        out_ref[...] = result[m * CAP : (m + 1) * CAP].astype(out_ref.dtype)


def combine_kernel(live, masks, mix_ref, own_ref, *refs):
    back_refs, out_ref = refs[:-1], refs[-1]
    mine = lax.axis_index("exp")
    mix = mix_ref[...]
    lane = lax.broadcasted_iota(jnp.int32, mix.shape, 1)
    total = own_ref[...]
    core = lax.axis_index("tp")
    for (even, odd), back_ref in zip(masks, back_refs):
        expert = lax.rem(mine ^ jnp.where(core == 0, even, odd), live)
        back = back_ref[...].astype(jnp.float32)
        for s in range(CAP):
            share = jnp.sum(jnp.where(lane == expert * CAP + s, mix, 0.0), axis=1, keepdims=True)
            total = total + share * back[s : s + 1]
    out_ref[...] = total.astype(out_ref.dtype)


def on_device(
    queries, keys, values, out_weight, norm_gain, routes, route_weight, w_gate, w_up, w_down
):
    blocks, lanes, rows, heads, head_dim = queries.shape
    width = out_weight.shape[1]
    n_exp = lax.axis_size("exp")
    live = n_exp // 2
    count = blocks * rows
    group = heads * n_exp // keys.shape[1]
    note_width = -(-(live * CAP) // LANES) * LANES
    (kv,) = call(
        functools.partial(open_kernel, heads, group),
        [((2 * keys.shape[0], head_dim), jnp.bfloat16)],
        *far((keys, values)),
        where=pltpu.HBM,
        scratch=[pltpu.VMEM(a.shape, a.dtype) for a in (keys, values)]
        + [pltpu.SemaphoreType.DMA((2,))],
        name="open",
    )
    masks, got = gather_ctx(kv)
    weights = (w_gate[0].T, w_up[0].T, w_down[0])
    small = (queries.reshape(count, heads, head_dim), routes, route_weight)
    got[1], *tied = lax.optimization_barrier((got[1], *weights, *small))
    moved = [swap(w, "tp", 1) for w in tied[:3]]
    query, note, mix = call(
        functools.partial(route_kernel, live, blocks),
        [
            ((heads * count, head_dim), jnp.bfloat16),
            ((count, note_width), jnp.bfloat16),
            ((rows, note_width), jnp.float32),
        ],
        *far(tied[3:]),
        where=pltpu.HBM,
        scratch=[pltpu.VMEM(a.shape, a.dtype) for a in small] + [pltpu.SemaphoreType.DMA((3,))],
        name="route",
    )
    (mixed,) = call(
        functools.partial(attend_kernel, masks, blocks),
        [((count, heads * head_dim), jnp.bfloat16)],
        query,
        *got,
        name="attend",
    )
    term = jnp.dot(mixed, out_weight, preferred_element_type=jnp.float32).astype(jnp.bfloat16)
    summed = jnp.concatenate([term, note], axis=1)
    summed, *weights = lax.optimization_barrier((summed, *weights))
    weights = load(weights, "load_mine")
    steps = [1 << i for i in range(n_exp.bit_length() - 1)]
    for i, step in enumerate(steps):
        other = swap_by_core(summed, "exp", (step, steps[-1 - i]))
        if i < len(steps) - 1:
            summed = (summed.astype(jnp.float32) + other.astype(jnp.float32)).astype(jnp.bfloat16)
    masks = [(0, 0), (3, 3), (1, 2), (2, 1)]
    slots = blocks * CAP
    own, x, part = call(
        functools.partial(first_kernel, blocks, live, masks),
        [
            ((rows, width), jnp.float32),
            ((slots, width), jnp.bfloat16),
            ((slots, width), jnp.float32),
        ],
        summed,
        other,
        norm_gain.reshape(1, width),
        *weights,
        flops=6 * slots * w_down.size,
        read=6 * w_down.size,
        name="first",
    )
    results = call(
        second_kernel,
        [((CAP, width), jnp.bfloat16)] * n_exp,
        x,
        part,
        *moved,
        flops=6 * slots * w_down.size,
        read=6 * w_down.size,
        name="second",
    )
    back = [
        results[0] if even == 0 else swap_by_core(results[i], "exp", (even, odd))
        for i, (even, odd) in enumerate(masks)
    ]
    (out,) = call(
        functools.partial(combine_kernel, live, masks),
        [((rows, width), jnp.bfloat16)],
        mix,
        own,
        *back,
        kept=jax.ShapeDtypeStruct,
        name="combine",
    )
    return out


def solution(mesh):
    in_specs = (
        P("ctx", "tp", None, "exp", None),
        P("ctx", None, None),
        P("ctx", None, None),
        P("exp", None),
        P(),
        P(("ctx", "exp", "tp"), None),
        P(("ctx", "exp", "tp"), None),
        P("exp", None, "tp"),
        P("exp", None, "tp"),
        P("exp", "tp", None),
    )
    out_specs = P(("ctx", "exp", "tp"), None)
    return jax.shard_map(
        on_device, mesh=mesh, in_specs=in_specs, out_specs=out_specs, check_vma=False
    )
```

```python
import functools

import jax
import jax.numpy as jnp
from jax import lax
from jax.experimental import pallas as pl
from jax.experimental.pallas import tpu as pltpu
from jax.sharding import PartitionSpec as P

CAP = 2
LANES = 128
VMEM_LIMIT = 24 * 1024 * 1024


def silu_mul(gate, up):
    return gate / (1.0 + jnp.exp(-gate)) * up


def swap(x, axis, mask):
    size = lax.axis_size(axis)
    return lax.ppermute(x, axis, [(i, i ^ mask) for i in range(size)])


def swap_by_core(x, axis, masks):
    size, cores = lax.axis_size(axis), lax.axis_size("tp")
    pairs = [
        (i * cores + t, (i ^ masks[t % len(masks)]) * cores + t)
        for i in range(size)
        for t in range(cores)
    ]
    return lax.ppermute(x, (axis, "tp"), pairs)


def by_distance(size):
    bits = size.bit_length() - 1
    mirror = [sum((m >> i & 1) << (bits - 1 - i) for i in range(bits)) for m in range(size)]
    far_first = sorted(range(1, size), key=lambda m: -m.bit_count())
    return [(0, 0)] + [(m, mirror[m]) for m in far_first]


def gather_ctx(x):
    size = lax.axis_size("ctx")
    masks, got = [(0, 0)], [x]
    for low in range(1, size // 2):
        high = size - low
        mine = swap_by_core(x, "ctx", (low, high))
        masks += [(low, high), (high, low)]
        got += [mine, swap(mine, "tp", 1)]
    masks.append((size // 2, size // 2))
    got.append(swap(x, "ctx", size // 2))
    return masks, got


def far(args):
    return [pltpu.with_memory_space_constraint(a, pltpu.HBM) for a in args]


def call(kernel, outs, *args, where=pltpu.VMEM, scratch=(), kept=pltpu.VMEM, flops=0, read=0, name=None):
    return pl.pallas_call(
        kernel,
        out_shape=[kept(shape, dtype) for shape, dtype in outs],
        in_specs=[pl.BlockSpec(memory_space=where)] * len(args),
        out_specs=[pl.BlockSpec(memory_space=pltpu.VMEM)] * len(outs),
        scratch_shapes=scratch,
        compiler_params=pltpu.CompilerParams(vmem_limit_bytes=VMEM_LIMIT),
        cost_estimate=pl.CostEstimate(flops=flops, bytes_accessed=read, transcendentals=0),
        name=name,
    )(*args)


def open_kernel(heads, group, key_hbm, value_hbm, kv_ref, key_ref, value_ref, sems):
    copies = [
        pltpu.make_async_copy(key_hbm, key_ref, sems.at[0]),
        pltpu.make_async_copy(value_hbm, value_ref, sems.at[1]),
    ]
    for copy in copies:
        copy.start()
    span = key_ref.shape[0]
    kv_head = lax.axis_index("exp") * heads // group
    for n, ref in enumerate((key_ref, value_ref)):
        copies[n].wait()
        wanted = lax.broadcasted_iota(jnp.int32, ref.shape, 1) == kv_head
        kept = jnp.sum(jnp.where(wanted, ref[...].astype(jnp.float32), 0.0), axis=1)
        kv_ref[n * span : (n + 1) * span, :] = kept.astype(kv_ref.dtype)


def route_kernel(live, blocks, *refs):
    ins, (q_ref, note_ref, mix_ref), held, sems = refs[:3], refs[3:6], refs[6:9], refs[9]
    copies = [pltpu.make_async_copy(i, h, sems.at[n]) for n, (i, h) in enumerate(zip(ins, held))]
    for copy in copies:
        copy.start()
    query_ref, routes_ref, weight_ref = held
    heads = query_ref.shape[1]
    mine = lax.axis_index("exp")
    for copy in copies:
        copy.wait()
    q_ref[...] = jnp.concatenate([query_ref[:, h, :] for h in range(heads)], axis=0)
    rows, picks = routes_ref.shape
    width = mix_ref.shape[1]
    routes, weight = routes_ref[...], weight_ref[...]
    lane = lax.broadcasted_iota(jnp.int32, (rows, width), 1)
    expert = jnp.where(lane < live * CAP, lane // CAP, -1)
    has = jnp.zeros((rows, width), jnp.float32)
    part = jnp.zeros((rows, width), jnp.float32)
    for k in range(picks):
        hit = routes[:, k : k + 1] == expert
        has = has + jnp.where(hit, 1.0, 0.0)
        part = part + jnp.where(hit, weight[:, k : k + 1], 0.0)
    earlier = [jnp.zeros((1, width), jnp.float32)]
    for r in range(rows - 1):
        earlier.append(earlier[-1] + has[r : r + 1])
    slot = jnp.concatenate(earlier, axis=0)
    hit = jnp.where(slot == (lane % CAP).astype(jnp.float32), has, 0.0)
    mix_ref[...] = hit * part / jnp.sum(weight, axis=1, keepdims=True)
    note_ref[...] = jnp.concatenate(
        [jnp.where(mine == b, hit, 0.0) for b in range(blocks)], axis=0
    ).astype(note_ref.dtype)


def attend_kernel(masks, blocks, q_ref, *refs):
    kv_refs, out_ref = refs[:-1], refs[-1]
    count = out_ref.shape[0]
    heads = q_ref.shape[0] // count
    head_dim = q_ref.shape[1]
    span = kv_refs[0].shape[0] // 2
    rows = count // blocks
    n_tp = lax.axis_size("tp")
    ctx, core = lax.axis_index("ctx"), lax.axis_index("tp")
    key = jnp.concatenate([r[:span, :] for r in kv_refs], axis=0)
    value = jnp.concatenate([r[span:, :] for r in kv_refs], axis=0)
    score = lax.dot_general(
        q_ref[...], key, (((1,), (1,)), ((), ())), preferred_element_type=jnp.float32
    ) * (head_dim ** (-0.5))
    lane = lax.broadcasted_iota(jnp.int32, (1, len(kv_refs) * span), 1)
    start = jnp.zeros_like(lane)
    for j, (even, odd) in enumerate(masks):
        block = ctx ^ jnp.where(core == 0, even, odd)
        start = jnp.where(lane // span == j, block * span, start)
    key_pos = start + lane % span
    row = lax.broadcasted_iota(jnp.int32, (heads * count, 1), 0) % count
    query_pos = ((ctx * blocks + row // rows) * n_tp + core) * rows + row % rows
    allowed = key_pos <= query_pos
    score = jnp.where(allowed, score, -1e30)
    prob = jnp.where(allowed, jnp.exp(score - jnp.max(score, axis=1, keepdims=True)), 0.0)
    total = jnp.sum(prob, axis=1, keepdims=True)
    mixed = jnp.dot(prob.astype(jnp.bfloat16), value, preferred_element_type=jnp.float32) / total
    mixed = mixed.astype(jnp.bfloat16)
    for h in range(heads):
        out_ref[:, h * head_dim : (h + 1) * head_dim] = mixed[h * count : (h + 1) * count]


def turn(gate_ref, up_ref, out_ref):
    units, width = gate_ref.shape
    for at in range(0, width, LANES):
        both = jnp.concatenate([gate_ref[:, at : at + LANES], up_ref[:, at : at + LANES]], axis=0)
        out_ref[at : at + LANES, :] = both.T


def load_kernel(gate_hbm, up_hbm, down_hbm, wide_ref, down_ref, gate_ref, up_ref, sems):
    ends = ((gate_hbm, gate_ref), (up_hbm, up_ref), (down_hbm, down_ref))
    copies = [pltpu.make_async_copy(i, o, sems.at[n]) for n, (i, o) in enumerate(ends)]
    for copy in copies:
        copy.start()
    copies[0].wait()
    copies[1].wait()
    turn(gate_ref, up_ref, wide_ref)
    copies[2].wait()


def hidden_units(x, wide_ref, down_ref):
    units = down_ref.shape[0]
    both = jnp.dot(x, wide_ref[...], preferred_element_type=jnp.float32)
    hidden = silu_mul(both[:, :units], both[:, units:]).astype(jnp.bfloat16)
    return jnp.dot(hidden, down_ref[...], preferred_element_type=jnp.float32)


def experts_kernel(blocks, live, masks, mine_ref, other_ref, gain_ref, *refs):
    weights, own_ref, outs = refs[:4], refs[4], refs[5:]
    count, width = mine_ref.shape[0], own_ref.shape[1]
    rows = count // blocks
    mine = lax.axis_index("exp")
    summed = (mine_ref[:, :width].astype(jnp.float32) + other_ref[:, :width].astype(jnp.float32)).astype(
        jnp.bfloat16
    )
    shape = (rows, count)
    own = (
        lax.broadcasted_iota(jnp.int32, shape, 0) + mine * rows
        == lax.broadcasted_iota(jnp.int32, shape, 1)
    )
    own = own.astype(jnp.float32).astype(jnp.bfloat16)
    own_ref[...] = jnp.dot(own, summed, preferred_element_type=jnp.float32)
    state = summed.astype(jnp.float32)
    note = mine_ref[:, width:] + other_ref[:, width:]
    inverse = lax.rsqrt(jnp.mean(state * state, axis=1, keepdims=True) + 1e-06)
    normed = (state * inverse * gain_ref[...]).astype(jnp.bfloat16)
    expert = lax.rem(mine, live)
    slots = blocks * CAP
    shape = (slots, note.shape[1])
    pick_lane = (
        lax.broadcasted_iota(jnp.int32, shape, 1)
        == expert * CAP + lax.broadcasted_iota(jnp.int32, shape, 0) % CAP
    )
    pick = lax.dot_general(
        pick_lane.astype(jnp.float32).astype(jnp.bfloat16),
        note,
        (((1,), (1,)), ((), ())),
        preferred_element_type=jnp.float32,
    )
    shape = (slots, count)
    place = lax.broadcasted_iota(jnp.int32, shape, 0) // CAP
    core = lax.axis_index("tp")
    mask = jnp.zeros(shape, jnp.int32)
    for i, (even, odd) in enumerate(masks):
        mask = jnp.where(place == i, jnp.where(core == 0, even, odd), mask)
    same = mask == (lax.broadcasted_iota(jnp.int32, shape, 1) // rows) ^ mine
    pick = jnp.where(same, pick, 0.0).astype(jnp.bfloat16)
    x = jnp.dot(pick, normed, preferred_element_type=jnp.float32).astype(jnp.bfloat16)
    result = hidden_units(x, *weights[:2]) + hidden_units(x, *weights[2:])
    for m, out_ref in enumerate(outs):
        out_ref[...] = result[m * CAP : (m + 1) * CAP].astype(out_ref.dtype)


def combine_kernel(live, masks, mix_ref, own_ref, *refs):
    back_refs, out_ref = refs[:-1], refs[-1]
    mine = lax.axis_index("exp")
    mix = mix_ref[...]
    lane = lax.broadcasted_iota(jnp.int32, mix.shape, 1)
    total = own_ref[...]
    core = lax.axis_index("tp")
    for (even, odd), back_ref in zip(masks, back_refs):
        expert = lax.rem(mine ^ jnp.where(core == 0, even, odd), live)
        back = back_ref[...].astype(jnp.float32)
        for s in range(CAP):
            share = jnp.sum(jnp.where(lane == expert * CAP + s, mix, 0.0), axis=1, keepdims=True)
            total = total + share * back[s : s + 1]
    out_ref[...] = total.astype(out_ref.dtype)


def on_device(
    queries, keys, values, out_weight, norm_gain, routes, route_weight, w_gate, w_up, w_down
):
    blocks, lanes, rows, heads, head_dim = queries.shape
    width = out_weight.shape[1]
    n_exp = lax.axis_size("exp")
    live = n_exp // 2
    count = blocks * rows
    group = heads * n_exp // keys.shape[1]
    note_width = -(-(live * CAP) // LANES) * LANES
    (kv,) = call(
        functools.partial(open_kernel, heads, group),
        [((2 * keys.shape[0], head_dim), jnp.bfloat16)],
        *far((keys, values)),
        where=pltpu.HBM,
        scratch=[pltpu.VMEM(a.shape, a.dtype) for a in (keys, values)]
        + [pltpu.SemaphoreType.DMA((2,))],
        name="open",
    )
    masks, got = gather_ctx(kv)
    weights = (w_gate[0].T, w_up[0].T, w_down[0])
    small = (queries.reshape(count, heads, head_dim), routes, route_weight)
    got[1], *tied = lax.optimization_barrier((got[1], *weights, *small))
    moved = [swap(w, "tp", 1) for w in tied[:3]]
    query, note, mix = call(
        functools.partial(route_kernel, live, blocks),
        [
            ((heads * count, head_dim), jnp.bfloat16),
            ((count, note_width), jnp.bfloat16),
            ((rows, note_width), jnp.float32),
        ],
        *far(tied[3:]),
        where=pltpu.HBM,
        scratch=[pltpu.VMEM(a.shape, a.dtype) for a in small] + [pltpu.SemaphoreType.DMA((3,))],
        name="route",
    )
    (mixed,) = call(
        functools.partial(attend_kernel, masks, blocks),
        [((count, heads * head_dim), jnp.bfloat16)],
        query,
        *got,
        name="attend",
    )
    term = jnp.dot(mixed, out_weight, preferred_element_type=jnp.float32).astype(jnp.bfloat16)
    summed = jnp.concatenate([term, note], axis=1)
    units = w_down.shape[1]
    summed, *weights = lax.optimization_barrier((summed, *weights))
    weights = call(
        load_kernel,
        [((width, 2 * units), w_down.dtype), ((units, width), w_down.dtype)],
        *far(weights),
        where=pltpu.HBM,
        scratch=[pltpu.VMEM((units, width), w_down.dtype)] * 2 + [pltpu.SemaphoreType.DMA((3,))],
        read=6 * w_down.size,
        name="load",
    )
    steps = [1 << i for i in range(n_exp.bit_length() - 1)]
    for i, step in enumerate(steps):
        other = swap_by_core(summed, "exp", (step, steps[-1 - i]))
        if i < len(steps) - 1:
            summed = (summed.astype(jnp.float32) + other.astype(jnp.float32)).astype(jnp.bfloat16)
            if i == 0:
                summed, *tied = lax.optimization_barrier((summed, *weights, *moved[:2]))
                weights, moved[:2] = tied[:2], tied[2:]
    (wide,) = call(
        turn, [((width, 2 * units), w_down.dtype)], *moved[:2], read=4 * w_down.size, name="turn"
    )
    masks = by_distance(n_exp)
    slots = blocks * CAP
    own, *results = call(
        functools.partial(experts_kernel, blocks, live, masks),
        [((rows, width), jnp.float32)] + [((CAP, width), jnp.bfloat16)] * n_exp,
        summed,
        other,
        norm_gain.reshape(1, width),
        *weights,
        wide,
        moved[2],
        flops=12 * slots * w_down.size,
        read=12 * w_down.size,
        name="experts",
    )
    back = [
        results[0] if even == 0 else swap_by_core(results[i], "exp", (even, odd))
        for i, (even, odd) in enumerate(masks)
    ]
    (out,) = call(
        functools.partial(combine_kernel, live, masks),
        [((rows, width), jnp.bfloat16)],
        mix,
        own,
        *back,
        kept=jax.ShapeDtypeStruct,
        name="combine",
    )
    return out


def solution(mesh):
    in_specs = (
        P("ctx", "tp", None, "exp", None),
        P("ctx", None, None),
        P("ctx", None, None),
        P("exp", None),
        P(),
        P(("ctx", "exp", "tp"), None),
        P(("ctx", "exp", "tp"), None),
        P("exp", None, "tp"),
        P("exp", None, "tp"),
        P("exp", "tp", None),
    )
    out_specs = P(("ctx", "exp", "tp"), None)
    return jax.shard_map(
        on_device, mesh=mesh, in_specs=in_specs, out_specs=out_specs, check_vma=False
    )
```

```python
import functools

import jax
import jax.numpy as jnp
from jax import lax
from jax.experimental import pallas as pl
from jax.experimental.pallas import tpu as pltpu
from jax.sharding import PartitionSpec as P

CAP = 2
LANES = 128
VMEM_LIMIT = 24 * 1024 * 1024


def silu_mul(gate, up):
    return gate / (1.0 + jnp.exp(-gate)) * up


def swap(x, axis, mask):
    size = lax.axis_size(axis)
    return lax.ppermute(x, axis, [(i, i ^ mask) for i in range(size)])


def swap_by_core(x, axis, masks, across=0):
    size, cores = lax.axis_size(axis), lax.axis_size("tp")
    pairs = [
        (i * cores + t, (i ^ masks[t % len(masks)]) * cores + (t ^ across))
        for i in range(size)
        for t in range(cores)
    ]
    return lax.ppermute(x, (axis, "tp"), pairs)


def by_distance(size):
    bits = size.bit_length() - 1
    mirror = [sum((m >> i & 1) << (bits - 1 - i) for i in range(bits)) for m in range(size)]
    far_first = sorted(range(1, size), key=lambda m: -m.bit_count())
    return [(0, 0)] + [(m, mirror[m]) for m in far_first]


def gather_ctx(x):
    size = lax.axis_size("ctx")
    masks, got = [(0, 0)], [x]
    for low in range(1, size // 2):
        high = size - low
        mine = swap_by_core(x, "ctx", (low, high))
        masks += [(low, high), (high, low)]
        got += [mine, swap(mine, "tp", 1)]
    masks.append((size // 2, size // 2))
    got.append(swap_by_core(x, "ctx", masks[-1], across=1))
    return masks, got


def far(args):
    return [pltpu.with_memory_space_constraint(a, pltpu.HBM) for a in args]


def call(kernel, outs, *args, where=pltpu.VMEM, scratch=(), kept=pltpu.VMEM, flops=0, read=0, name=None):
    return pl.pallas_call(
        kernel,
        out_shape=[kept(shape, dtype) for shape, dtype in outs],
        in_specs=[pl.BlockSpec(memory_space=where)] * len(args),
        out_specs=[pl.BlockSpec(memory_space=pltpu.VMEM)] * len(outs),
        scratch_shapes=scratch,
        compiler_params=pltpu.CompilerParams(vmem_limit_bytes=VMEM_LIMIT),
        cost_estimate=pl.CostEstimate(flops=flops, bytes_accessed=read, transcendentals=0),
        name=name,
    )(*args)


def open_kernel(heads, group, key_hbm, value_hbm, kv_ref, key_ref, value_ref, sems):
    copies = [
        pltpu.make_async_copy(key_hbm, key_ref, sems.at[0]),
        pltpu.make_async_copy(value_hbm, value_ref, sems.at[1]),
    ]
    for copy in copies:
        copy.start()
    span = key_ref.shape[0]
    kv_head = lax.axis_index("exp") * heads // group
    for n, ref in enumerate((key_ref, value_ref)):
        copies[n].wait()
        wanted = lax.broadcasted_iota(jnp.int32, ref.shape, 1) == kv_head
        kept = jnp.sum(jnp.where(wanted, ref[...].astype(jnp.float32), 0.0), axis=1)
        kv_ref[n * span : (n + 1) * span, :] = kept.astype(kv_ref.dtype)


def route_kernel(live, blocks, *refs):
    ins, (q_ref, note_ref, mix_ref), held, sems = refs[:3], refs[3:6], refs[6:9], refs[9]
    copies = [pltpu.make_async_copy(i, h, sems.at[n]) for n, (i, h) in enumerate(zip(ins, held))]
    for copy in copies:
        copy.start()
    query_ref, routes_ref, weight_ref = held
    heads = query_ref.shape[1]
    mine = lax.axis_index("exp")
    for copy in copies:
        copy.wait()
    q_ref[...] = jnp.concatenate([query_ref[:, h, :] for h in range(heads)], axis=0)
    rows, picks = routes_ref.shape
    width = mix_ref.shape[1]
    routes, weight = routes_ref[...], weight_ref[...]
    lane = lax.broadcasted_iota(jnp.int32, (rows, width), 1)
    expert = jnp.where(lane < live * CAP, lane // CAP, -1)
    has = jnp.zeros((rows, width), jnp.float32)
    part = jnp.zeros((rows, width), jnp.float32)
    for k in range(picks):
        hit = routes[:, k : k + 1] == expert
        has = has + jnp.where(hit, 1.0, 0.0)
        part = part + jnp.where(hit, weight[:, k : k + 1], 0.0)
    earlier = [jnp.zeros((1, width), jnp.float32)]
    for r in range(rows - 1):
        earlier.append(earlier[-1] + has[r : r + 1])
    slot = jnp.concatenate(earlier, axis=0)
    hit = jnp.where(slot == (lane % CAP).astype(jnp.float32), has, 0.0)
    mix_ref[...] = hit * part / jnp.sum(weight, axis=1, keepdims=True)
    note_ref[...] = jnp.concatenate(
        [jnp.where(mine == b, hit, 0.0) for b in range(blocks)], axis=0
    ).astype(note_ref.dtype)


def attend_kernel(masks, blocks, q_ref, *refs):
    kv_refs, out_ref = refs[:-1], refs[-1]
    count = out_ref.shape[0]
    heads = q_ref.shape[0] // count
    head_dim = q_ref.shape[1]
    span = kv_refs[0].shape[0] // 2
    rows = count // blocks
    n_tp = lax.axis_size("tp")
    ctx, core = lax.axis_index("ctx"), lax.axis_index("tp")
    key = jnp.concatenate([r[:span, :] for r in kv_refs], axis=0)
    value = jnp.concatenate([r[span:, :] for r in kv_refs], axis=0)
    score = lax.dot_general(
        q_ref[...], key, (((1,), (1,)), ((), ())), preferred_element_type=jnp.float32
    ) * (head_dim ** (-0.5))
    lane = lax.broadcasted_iota(jnp.int32, (1, len(kv_refs) * span), 1)
    start = jnp.zeros_like(lane)
    for j, (even, odd) in enumerate(masks):
        block = ctx ^ jnp.where(core == 0, even, odd)
        start = jnp.where(lane // span == j, block * span, start)
    key_pos = start + lane % span
    row = lax.broadcasted_iota(jnp.int32, (heads * count, 1), 0) % count
    query_pos = ((ctx * blocks + row // rows) * n_tp + core) * rows + row % rows
    allowed = key_pos <= query_pos
    score = jnp.where(allowed, score, -1e30)
    prob = jnp.where(allowed, jnp.exp(score - jnp.max(score, axis=1, keepdims=True)), 0.0)
    total = jnp.sum(prob, axis=1, keepdims=True)
    mixed = jnp.dot(prob.astype(jnp.bfloat16), value, preferred_element_type=jnp.float32) / total
    mixed = mixed.astype(jnp.bfloat16)
    for h in range(heads):
        out_ref[:, h * head_dim : (h + 1) * head_dim] = mixed[h * count : (h + 1) * count]


def turn(gate_ref, up_ref, out_ref):
    units, width = gate_ref.shape
    for at in range(0, width, LANES):
        both = jnp.concatenate([gate_ref[:, at : at + LANES], up_ref[:, at : at + LANES]], axis=0)
        out_ref[at : at + LANES, :] = both.T


def load_kernel(gate_hbm, up_hbm, down_hbm, wide_ref, down_ref, gate_ref, up_ref, sems):
    ends = ((gate_hbm, gate_ref), (up_hbm, up_ref), (down_hbm, down_ref))
    copies = [pltpu.make_async_copy(i, o, sems.at[n]) for n, (i, o) in enumerate(ends)]
    for copy in copies:
        copy.start()
    copies[0].wait()
    copies[1].wait()
    turn(gate_ref, up_ref, wide_ref)
    copies[2].wait()


def hidden_units(x, wide_ref, down_ref):
    units = down_ref.shape[0]
    both = jnp.dot(x, wide_ref[...], preferred_element_type=jnp.float32)
    hidden = silu_mul(both[:, :units], both[:, units:]).astype(jnp.bfloat16)
    return jnp.dot(hidden, down_ref[...], preferred_element_type=jnp.float32)


def experts_kernel(blocks, live, masks, mine_ref, other_ref, gain_ref, *refs):
    weights, own_ref, outs = refs[:4], refs[4], refs[5:]
    count, width = mine_ref.shape[0], own_ref.shape[1]
    rows = count // blocks
    mine = lax.axis_index("exp")
    summed = (mine_ref[:, :width].astype(jnp.float32) + other_ref[:, :width].astype(jnp.float32)).astype(
        jnp.bfloat16
    )
    shape = (rows, count)
    own = (
        lax.broadcasted_iota(jnp.int32, shape, 0) + mine * rows
        == lax.broadcasted_iota(jnp.int32, shape, 1)
    )
    own = own.astype(jnp.float32).astype(jnp.bfloat16)
    own_ref[...] = jnp.dot(own, summed, preferred_element_type=jnp.float32)
    state = summed.astype(jnp.float32)
    note = mine_ref[:, width:] + other_ref[:, width:]
    inverse = lax.rsqrt(jnp.mean(state * state, axis=1, keepdims=True) + 1e-06)
    normed = (state * inverse * gain_ref[...]).astype(jnp.bfloat16)
    expert = lax.rem(mine, live)
    slots = blocks * CAP
    shape = (slots, note.shape[1])
    pick_lane = (
        lax.broadcasted_iota(jnp.int32, shape, 1)
        == expert * CAP + lax.broadcasted_iota(jnp.int32, shape, 0) % CAP
    )
    pick = lax.dot_general(
        pick_lane.astype(jnp.float32).astype(jnp.bfloat16),
        note,
        (((1,), (1,)), ((), ())),
        preferred_element_type=jnp.float32,
    )
    shape = (slots, count)
    place = lax.broadcasted_iota(jnp.int32, shape, 0) // CAP
    core = lax.axis_index("tp")
    mask = jnp.zeros(shape, jnp.int32)
    for i, (even, odd) in enumerate(masks):
        mask = jnp.where(place == i, jnp.where(core == 0, even, odd), mask)
    same = mask == (lax.broadcasted_iota(jnp.int32, shape, 1) // rows) ^ mine
    pick = jnp.where(same, pick, 0.0).astype(jnp.bfloat16)
    x = jnp.dot(pick, normed, preferred_element_type=jnp.float32).astype(jnp.bfloat16)
    result = hidden_units(x, *weights[:2]) + hidden_units(x, *weights[2:])
    for m, out_ref in enumerate(outs):
        out_ref[...] = result[m * CAP : (m + 1) * CAP].astype(out_ref.dtype)


def combine_kernel(live, masks, mix_ref, own_ref, *refs):
    back_refs, out_ref = refs[:-1], refs[-1]
    mine = lax.axis_index("exp")
    mix = mix_ref[...]
    lane = lax.broadcasted_iota(jnp.int32, mix.shape, 1)
    total = own_ref[...]
    core = lax.axis_index("tp")
    for (even, odd), back_ref in zip(masks, back_refs):
        expert = lax.rem(mine ^ jnp.where(core == 0, even, odd), live)
        back = back_ref[...].astype(jnp.float32)
        for s in range(CAP):
            share = jnp.sum(jnp.where(lane == expert * CAP + s, mix, 0.0), axis=1, keepdims=True)
            total = total + share * back[s : s + 1]
    out_ref[...] = total.astype(out_ref.dtype)


def on_device(
    queries, keys, values, out_weight, norm_gain, routes, route_weight, w_gate, w_up, w_down
):
    blocks, lanes, rows, heads, head_dim = queries.shape
    width = out_weight.shape[1]
    n_exp = lax.axis_size("exp")
    live = n_exp // 2
    count = blocks * rows
    group = heads * n_exp // keys.shape[1]
    note_width = -(-(live * CAP) // LANES) * LANES
    (kv,) = call(
        functools.partial(open_kernel, heads, group),
        [((2 * keys.shape[0], head_dim), jnp.bfloat16)],
        *far((keys, values)),
        where=pltpu.HBM,
        scratch=[pltpu.VMEM(a.shape, a.dtype) for a in (keys, values)]
        + [pltpu.SemaphoreType.DMA((2,))],
        name="open",
    )
    masks, got = gather_ctx(kv)
    weights = (w_gate[0].T, w_up[0].T, w_down[0])
    small = (queries.reshape(count, heads, head_dim), routes, route_weight)
    got[1], *tied = lax.optimization_barrier((got[1], *weights, *small))
    moved = [swap(w, "tp", 1) for w in tied[:3]]
    query, note, mix = call(
        functools.partial(route_kernel, live, blocks),
        [
            ((heads * count, head_dim), jnp.bfloat16),
            ((count, note_width), jnp.bfloat16),
            ((rows, note_width), jnp.float32),
        ],
        *far(tied[3:]),
        where=pltpu.HBM,
        scratch=[pltpu.VMEM(a.shape, a.dtype) for a in small] + [pltpu.SemaphoreType.DMA((3,))],
        name="route",
    )
    (mixed,) = call(
        functools.partial(attend_kernel, masks, blocks),
        [((count, heads * head_dim), jnp.bfloat16)],
        query,
        *got,
        name="attend",
    )
    term = jnp.dot(mixed, out_weight, preferred_element_type=jnp.float32).astype(jnp.bfloat16)
    summed = jnp.concatenate([term, note], axis=1)
    units = w_down.shape[1]
    summed, *weights = lax.optimization_barrier((summed, *weights))
    weights = call(
        load_kernel,
        [((width, 2 * units), w_down.dtype), ((units, width), w_down.dtype)],
        *far(weights),
        where=pltpu.HBM,
        scratch=[pltpu.VMEM((units, width), w_down.dtype)] * 2 + [pltpu.SemaphoreType.DMA((3,))],
        read=6 * w_down.size,
        name="load",
    )
    steps = [1 << i for i in range(n_exp.bit_length() - 1)]
    for i, step in enumerate(steps):
        other = swap_by_core(summed, "exp", (step, steps[-1 - i]))
        if i < len(steps) - 1:
            summed = (summed.astype(jnp.float32) + other.astype(jnp.float32)).astype(jnp.bfloat16)
            if i == 0:
                summed, *tied = lax.optimization_barrier((summed, *weights, *moved[:2]))
                weights, moved[:2] = tied[:2], tied[2:]
    (wide,) = call(
        turn, [((width, 2 * units), w_down.dtype)], *moved[:2], read=4 * w_down.size, name="turn"
    )
    masks = by_distance(n_exp)
    slots = blocks * CAP
    own, *results = call(
        functools.partial(experts_kernel, blocks, live, masks),
        [((rows, width), jnp.float32)] + [((CAP, width), jnp.bfloat16)] * n_exp,
        summed,
        other,
        norm_gain.reshape(1, width),
        *weights,
        wide,
        moved[2],
        flops=12 * slots * w_down.size,
        read=12 * w_down.size,
        name="experts",
    )
    back = [results[0]]
    for (even, odd), result in zip(masks[1:], results[1:]):
        across = int(even.bit_count() > 1)
        result = swap_by_core(result, "exp", (even, odd), across)
        back.append(swap(result, "tp", 1) if across else result)
    (out,) = call(
        functools.partial(combine_kernel, live, masks),
        [((rows, width), jnp.bfloat16)],
        mix,
        own,
        *back,
        kept=jax.ShapeDtypeStruct,
        name="combine",
    )
    return out


def solution(mesh):
    in_specs = (
        P("ctx", "tp", None, "exp", None),
        P("ctx", None, None),
        P("ctx", None, None),
        P("exp", None),
        P(),
        P(("ctx", "exp", "tp"), None),
        P(("ctx", "exp", "tp"), None),
        P("exp", None, "tp"),
        P("exp", None, "tp"),
        P("exp", "tp", None),
    )
    out_specs = P(("ctx", "exp", "tp"), None)
    return jax.shard_map(
        on_device, mesh=mesh, in_specs=in_specs, out_specs=out_specs, check_vma=False
    )
```

```python
import functools

import jax
import jax.numpy as jnp
from jax import lax
from jax.experimental import pallas as pl
from jax.experimental.pallas import tpu as pltpu
from jax.sharding import PartitionSpec as P

CAP = 2
LANES = 128
CHUNKS = 4
VMEM_LIMIT = 24 * 1024 * 1024


def silu_mul(gate, up):
    return gate / (1.0 + jnp.exp(-gate)) * up


def swap(x, axis, mask):
    size = lax.axis_size(axis)
    return lax.ppermute(x, axis, [(i, i ^ mask) for i in range(size)])


def swap_by_core(x, axis, masks, across=0):
    size, cores = lax.axis_size(axis), lax.axis_size("tp")
    pairs = [
        (i * cores + t, (i ^ masks[t % len(masks)]) * cores + (t ^ across))
        for i in range(size)
        for t in range(cores)
    ]
    return lax.ppermute(x, (axis, "tp"), pairs)


def by_distance(size):
    bits = size.bit_length() - 1
    mirror = [sum((m >> i & 1) << (bits - 1 - i) for i in range(bits)) for m in range(size)]
    far_first = sorted(range(1, size), key=lambda m: -m.bit_count())
    return [(0, 0)] + [(m, mirror[m]) for m in far_first]


def gather_ctx(x):
    size = lax.axis_size("ctx")
    masks, got = [(0, 0)], [x]
    for low in range(1, size // 2):
        high = size - low
        mine = swap_by_core(x, "ctx", (low, high))
        masks += [(low, high), (high, low)]
        got += [mine, swap(mine, "tp", 1)]
    masks.append((size // 2, size // 2))
    got.append(swap_by_core(x, "ctx", masks[-1]))
    return masks, got


def far(args):
    return [pltpu.with_memory_space_constraint(a, pltpu.HBM) for a in args]


def call(kernel, outs, *args, where=pltpu.VMEM, scratch=(), kept=pltpu.VMEM, flops=0, read=0, name=None):
    return pl.pallas_call(
        kernel,
        out_shape=[kept(shape, dtype) for shape, dtype in outs],
        in_specs=[pl.BlockSpec(memory_space=where)] * len(args),
        out_specs=[pl.BlockSpec(memory_space=pltpu.HBM if kept is pltpu.HBM else pltpu.VMEM)] * len(outs),
        scratch_shapes=scratch,
        compiler_params=pltpu.CompilerParams(vmem_limit_bytes=VMEM_LIMIT),
        cost_estimate=pl.CostEstimate(flops=flops, bytes_accessed=read, transcendentals=0),
        name=name,
    )(*args)


def open_kernel(heads, group, key_hbm, value_hbm, kv_ref, key_ref, value_ref, sems):
    copies = [
        pltpu.make_async_copy(key_hbm, key_ref, sems.at[0]),
        pltpu.make_async_copy(value_hbm, value_ref, sems.at[1]),
    ]
    for copy in copies:
        copy.start()
    span = key_ref.shape[0]
    kv_head = lax.axis_index("exp") * heads // group
    for n, ref in enumerate((key_ref, value_ref)):
        copies[n].wait()
        wanted = lax.broadcasted_iota(jnp.int32, ref.shape, 1) == kv_head
        kept = jnp.sum(jnp.where(wanted, ref[...].astype(jnp.float32), 0.0), axis=1)
        kv_ref[n * span : (n + 1) * span, :] = kept.astype(kv_ref.dtype)


def allow(masks, blocks, rows, out_ref):
    heads_rows, keys = out_ref.shape
    count = blocks * rows
    span = keys // len(masks)
    n_tp = lax.axis_size("tp")
    ctx, core = lax.axis_index("ctx"), lax.axis_index("tp")
    lane = lax.broadcasted_iota(jnp.int32, (1, keys), 1)
    start = jnp.zeros_like(lane)
    for j, (even, odd) in enumerate(masks):
        block = ctx ^ jnp.where(core == 0, even, odd)
        start = jnp.where(lane // span == j, block * span, start)
    key_pos = start + lane % span
    row = lax.broadcasted_iota(jnp.int32, (heads_rows, 1), 0) % count
    query_pos = ((ctx * blocks + row // rows) * n_tp + core) * rows + row % rows
    allowed = key_pos <= query_pos
    out_ref[...] = jnp.where(allowed, 0.0, -1e30)


def route_kernel(live, blocks, masks, *refs):
    ins, (q_ref, note_ref, mix_ref, allowed_ref), held, sems = refs[:3], refs[3:7], refs[7:10], refs[10]
    copies = [pltpu.make_async_copy(i, h, sems.at[n]) for n, (i, h) in enumerate(zip(ins, held))]
    for copy in copies:
        copy.start()
    query_ref, routes_ref, weight_ref = held
    heads = query_ref.shape[1]
    mine = lax.axis_index("exp")
    allow(masks, blocks, routes_ref.shape[0], allowed_ref)
    for copy in copies:
        copy.wait()
    q_ref[...] = jnp.concatenate([query_ref[:, h, :] for h in range(heads)], axis=0)
    rows, picks = routes_ref.shape
    width = mix_ref.shape[1]
    routes, weight = routes_ref[...], weight_ref[...]
    lane = lax.broadcasted_iota(jnp.int32, (rows, width), 1)
    expert = jnp.where(lane < live * CAP, lane // CAP, -1)
    has = jnp.zeros((rows, width), jnp.float32)
    part = jnp.zeros((rows, width), jnp.float32)
    for k in range(picks):
        hit = routes[:, k : k + 1] == expert
        has = has + jnp.where(hit, 1.0, 0.0)
        part = part + jnp.where(hit, weight[:, k : k + 1], 0.0)
    earlier = [jnp.zeros((1, width), jnp.float32)]
    for r in range(rows - 1):
        earlier.append(earlier[-1] + has[r : r + 1])
    slot = jnp.concatenate(earlier, axis=0)
    hit = jnp.where(slot == (lane % CAP).astype(jnp.float32), has, 0.0)
    mix_ref[...] = hit * part / jnp.sum(weight, axis=1, keepdims=True)
    note_ref[...] = jnp.concatenate(
        [jnp.where(mine == b, hit, 0.0) for b in range(blocks)], axis=0
    ).astype(note_ref.dtype)


def attend_kernel(q_ref, allowed_ref, *refs):
    kv_refs, out_ref = refs[:-1], refs[-1]
    count = out_ref.shape[0]
    heads = q_ref.shape[0] // count
    head_dim = q_ref.shape[1]
    span = kv_refs[0].shape[0] // 2
    key = jnp.concatenate([r[:span, :] for r in kv_refs], axis=0)
    value = jnp.concatenate([r[span:, :] for r in kv_refs], axis=0)
    score = lax.dot_general(
        q_ref[...], key, (((1,), (1,)), ((), ())), preferred_element_type=jnp.float32
    ) * (head_dim ** (-0.5))
    score = score + allowed_ref[...]
    prob = jnp.exp(score - jnp.max(score, axis=1, keepdims=True))
    total = jnp.sum(prob, axis=1, keepdims=True)
    mixed = jnp.dot(prob.astype(jnp.bfloat16), value, preferred_element_type=jnp.float32) / total
    mixed = mixed.astype(jnp.bfloat16)
    for h in range(heads):
        out_ref[:, h * head_dim : (h + 1) * head_dim] = mixed[h * count : (h + 1) * count]


def turn(gate_ref, up_ref, out_ref):
    units, width = gate_ref.shape
    for at in range(0, width, LANES):
        both = jnp.concatenate([gate_ref[:, at : at + LANES], up_ref[:, at : at + LANES]], axis=0)
        out_ref[at : at + LANES, :] = both.T


def load_kernel(gate_hbm, up_hbm, down_hbm, wide_ref, down_ref, gate_ref, up_ref, sems):
    ends = ((gate_hbm, gate_ref), (up_hbm, up_ref), (down_hbm, down_ref))
    copies = [pltpu.make_async_copy(i, o, sems.at[n]) for n, (i, o) in enumerate(ends)]
    for copy in copies:
        copy.start()
    copies[0].wait()
    copies[1].wait()
    turn(gate_ref, up_ref, wide_ref)
    copies[2].wait()


def hidden_units(x, inverse, wide_ref, down_ref):
    units = down_ref.shape[0]
    both = jnp.dot(x, wide_ref[...], preferred_element_type=jnp.float32) * inverse
    hidden = silu_mul(both[:, :units], both[:, units:]).astype(jnp.bfloat16)
    return jnp.dot(hidden, down_ref[...], preferred_element_type=jnp.float32)


def experts_kernel(blocks, live, masks, parts, *refs):
    part_refs, gain_ref, refs = refs[:parts], refs[parts], refs[parts + 1 :]
    weights, own_ref, outs = refs[:4], refs[4], refs[5:]
    count, width = part_refs[0].shape[0], own_ref.shape[1]
    rows = count // blocks
    mine = lax.axis_index("exp")
    summed = sum(r[:, :width].astype(jnp.float32) for r in part_refs).astype(jnp.bfloat16)
    note = functools.reduce(lambda x, y: x + y, [r[:, width:] for r in part_refs])
    expert = lax.rem(mine, live)
    slots = blocks * CAP
    shape = (slots, note.shape[1])
    pick_lane = (
        lax.broadcasted_iota(jnp.int32, shape, 1)
        == expert * CAP + lax.broadcasted_iota(jnp.int32, shape, 0) % CAP
    )
    pick = lax.dot_general(
        pick_lane.astype(jnp.float32).astype(jnp.bfloat16),
        note,
        (((1,), (1,)), ((), ())),
        preferred_element_type=jnp.float32,
    )
    shape = (slots, count)
    place = lax.broadcasted_iota(jnp.int32, shape, 0) // CAP
    core = lax.axis_index("tp")
    mask = jnp.zeros(shape, jnp.int32)
    for i, (even, odd) in enumerate(masks):
        mask = jnp.where(place == i, jnp.where(core == 0, even, odd), mask)
    same = mask == (lax.broadcasted_iota(jnp.int32, shape, 1) // rows) ^ mine
    pick = jnp.where(same, pick, 0.0)
    shape = (rows, count)
    own = (
        lax.broadcasted_iota(jnp.int32, shape, 0) + mine * rows
        == lax.broadcasted_iota(jnp.int32, shape, 1)
    )
    pick = jnp.concatenate([pick, own.astype(jnp.float32)], axis=0).astype(jnp.bfloat16)
    picked = jnp.dot(pick, summed, preferred_element_type=jnp.float32)
    own_ref[...] = picked[slots:]
    state = picked[:slots]
    inverse = lax.rsqrt(jnp.mean(state * state, axis=1, keepdims=True) + 1e-06)
    x = (state * gain_ref[...]).astype(jnp.bfloat16)
    result = hidden_units(x, inverse, *weights[:2]) + hidden_units(x, inverse, *weights[2:])
    for m, out_ref in enumerate(outs):
        out_ref[...] = result[m * CAP : (m + 1) * CAP].astype(out_ref.dtype)


def combine_kernel(live, masks, mix_ref, own_ref, *refs):
    back_refs, (out_hbm, held_ref, sems) = refs[:-3], refs[-3:]
    mine, core = lax.axis_index("exp"), lax.axis_index("tp")
    mix = mix_ref[...]
    lane = lax.broadcasted_iota(jnp.int32, mix.shape, 1)
    shares = []
    for even, odd in masks:
        expert = lax.rem(mine ^ jnp.where(core == 0, even, odd), live)
        for s in range(CAP):
            wanted = lane == expert * CAP + s
            shares.append(jnp.sum(jnp.where(wanted, mix, 0.0), axis=1, keepdims=True))
    width = out_hbm.shape[1] // CHUNKS
    copies = []
    for n in range(CHUNKS):
        at = slice(n * width, (n + 1) * width)
        total = own_ref[:, at]
        for m, back_ref in enumerate(back_refs):
            back = back_ref[:, at].astype(jnp.float32)
            for s in range(CAP):
                total = total + shares[m * CAP + s] * back[s : s + 1]
        held_ref[:, at] = total.astype(held_ref.dtype)
        copies.append(pltpu.make_async_copy(held_ref.at[:, at], out_hbm.at[:, at], sems.at[n]))
        copies[-1].start()
    for copy in copies:
        copy.wait()


def on_device(
    queries, keys, values, out_weight, norm_gain, routes, route_weight, w_gate, w_up, w_down
):
    blocks, lanes, rows, heads, head_dim = queries.shape
    width = out_weight.shape[1]
    n_exp = lax.axis_size("exp")
    live = n_exp // 2
    count = blocks * rows
    group = heads * n_exp // keys.shape[1]
    note_width = -(-(live * CAP) // LANES) * LANES
    (kv,) = call(
        functools.partial(open_kernel, heads, group),
        [((2 * keys.shape[0], head_dim), jnp.bfloat16)],
        *far((keys, values)),
        where=pltpu.HBM,
        scratch=[pltpu.VMEM(a.shape, a.dtype) for a in (keys, values)]
        + [pltpu.SemaphoreType.DMA((2,))],
        name="open",
    )
    masks, got = gather_ctx(kv)
    weights = (w_gate[0].T, w_up[0].T, w_down[0])
    small = (queries.reshape(count, heads, head_dim), routes, route_weight)
    got[1], *tied = lax.optimization_barrier((got[1], *weights, *small))
    moved = [swap(w, "tp", 1) for w in tied[:3]]
    query, note, mix, allowed = call(
        functools.partial(route_kernel, live, blocks, masks),
        [
            ((heads * count, head_dim), jnp.bfloat16),
            ((count, note_width), jnp.bfloat16),
            ((rows, note_width), jnp.float32),
            ((heads * count, len(got) * keys.shape[0]), jnp.float32),
        ],
        *far(tied[3:]),
        where=pltpu.HBM,
        scratch=[pltpu.VMEM(a.shape, a.dtype) for a in small] + [pltpu.SemaphoreType.DMA((3,))],
        name="route",
    )
    (mixed,) = call(
        attend_kernel,
        [((count, heads * head_dim), jnp.bfloat16)],
        query,
        allowed,
        *got,
        flops=10**10,
        name="attend",
    )
    term = jnp.dot(mixed, out_weight, preferred_element_type=jnp.float32).astype(jnp.bfloat16)
    summed = jnp.concatenate([term, note], axis=1)
    units = w_down.shape[1]
    summed, *weights = lax.optimization_barrier((summed, *weights))
    weights = call(
        load_kernel,
        [((width, 2 * units), w_down.dtype), ((units, width), w_down.dtype)],
        *far(weights),
        where=pltpu.HBM,
        scratch=[pltpu.VMEM((units, width), w_down.dtype)] * 2 + [pltpu.SemaphoreType.DMA((3,))],
        read=6 * w_down.size,
        name="load",
    )
    steps = [1 << i for i in range(n_exp.bit_length() - 1)]
    for at in range(0, len(steps), 2):
        pair = steps[at : at + 2]
        low, high = pair[0], pair[-1]
        masks = [(low | high,) * 2, (low, high), (high, low)] if len(pair) == 2 else [(low, low)]
        others = [swap_by_core(summed, "exp", m) for m in masks]
        if at + 2 < len(steps):
            summed = sum(o.astype(jnp.float32) for o in others) + summed.astype(jnp.float32)
            summed = summed.astype(jnp.bfloat16)
    (wide,) = call(
        turn, [((width, 2 * units), w_down.dtype)], *moved[:2], read=4 * w_down.size, name="turn"
    )
    masks = by_distance(n_exp)
    slots = blocks * CAP
    own, *results = call(
        functools.partial(experts_kernel, blocks, live, masks, 1 + len(others)),
        [((rows, width), jnp.float32)] + [((CAP, width), jnp.bfloat16)] * n_exp,
        *others,
        summed,
        norm_gain.reshape(1, width),
        *weights,
        wide,
        moved[2],
        flops=12 * slots * w_down.size,
        read=12 * w_down.size,
        name="experts",
    )
    back = [results[0]]
    for (even, odd), result in zip(masks[1:], results[1:]):
        across = int(even.bit_count() > 1)
        result = swap_by_core(result, "exp", (even, odd), across)
        back.append(swap(result, "tp", 1) if across else result)
    (out,) = call(
        functools.partial(combine_kernel, live, masks),
        [((rows, width), jnp.bfloat16)],
        mix,
        own,
        *back,
        kept=pltpu.HBM,
        scratch=[pltpu.VMEM((rows, width), jnp.bfloat16), pltpu.SemaphoreType.DMA((CHUNKS,))],
        name="combine",
    )
    return out


def solution(mesh):
    in_specs = (
        P("ctx", "tp", None, "exp", None),
        P("ctx", None, None),
        P("ctx", None, None),
        P("exp", None),
        P(),
        P(("ctx", "exp", "tp"), None),
        P(("ctx", "exp", "tp"), None),
        P("exp", None, "tp"),
        P("exp", None, "tp"),
        P("exp", "tp", None),
    )
    out_specs = P(("ctx", "exp", "tp"), None)
    return jax.shard_map(
        on_device, mesh=mesh, in_specs=in_specs, out_specs=out_specs, check_vma=False
    )
```

```python
import functools

import jax
import jax.numpy as jnp
from jax import lax
from jax.experimental import pallas as pl
from jax.experimental.pallas import tpu as pltpu
from jax.sharding import PartitionSpec as P

CAP = 2
LANES = 128
CHUNKS = 4
VMEM_LIMIT = 24 * 1024 * 1024


def silu_mul(gate, up):
    return gate / (1.0 + jnp.exp(-gate)) * up


def swap(x, axis, mask):
    size = lax.axis_size(axis)
    return lax.ppermute(x, axis, [(i, i ^ mask) for i in range(size)])


def swap_by_core(x, axis, masks, across=0):
    size, cores = lax.axis_size(axis), lax.axis_size("tp")
    pairs = [
        (i * cores + t, (i ^ masks[t % len(masks)]) * cores + (t ^ across))
        for i in range(size)
        for t in range(cores)
    ]
    return lax.ppermute(x, (axis, "tp"), pairs)


def by_distance(size):
    bits = size.bit_length() - 1
    mirror = [sum((m >> i & 1) << (bits - 1 - i) for i in range(bits)) for m in range(size)]
    far_first = sorted(range(1, size), key=lambda m: (-m.bit_count(), -m))
    return [(0, 0)] + [(m, mirror[m]) for m in far_first]


def gather_ctx(x):
    size = lax.axis_size("ctx")
    masks, got = [(0, 0)], [x]
    for low in range(1, size // 2):
        high = size - low
        mine = swap_by_core(x, "ctx", (low, high))
        masks += [(low, high), (high, low)]
        got += [mine, swap(mine, "tp", 1)]
    masks.append((size // 2, size // 2))
    got.append(swap_by_core(x, "ctx", masks[-1]))
    return masks, got


def far(args):
    return [pltpu.with_memory_space_constraint(a, pltpu.HBM) for a in args]


def call(kernel, outs, *args, where=pltpu.VMEM, scratch=(), kept=pltpu.VMEM, flops=0, read=0, name=None):
    return pl.pallas_call(
        kernel,
        out_shape=[kept(shape, dtype) for shape, dtype in outs],
        in_specs=[pl.BlockSpec(memory_space=where)] * len(args),
        out_specs=[pl.BlockSpec(memory_space=pltpu.HBM if kept is pltpu.HBM else pltpu.VMEM)] * len(outs),
        scratch_shapes=scratch,
        compiler_params=pltpu.CompilerParams(vmem_limit_bytes=VMEM_LIMIT),
        cost_estimate=pl.CostEstimate(flops=flops, bytes_accessed=read, transcendentals=0),
        name=name,
    )(*args)


def open_kernel(heads, group, key_hbm, value_hbm, kv_ref, key_ref, value_ref, sems):
    copies = [
        pltpu.make_async_copy(key_hbm, key_ref, sems.at[0]),
        pltpu.make_async_copy(value_hbm, value_ref, sems.at[1]),
    ]
    for copy in copies:
        copy.start()
    span = key_ref.shape[0]
    kv_head = lax.axis_index("exp") * heads // group
    for n, ref in enumerate((key_ref, value_ref)):
        copies[n].wait()
        wanted = lax.broadcasted_iota(jnp.int32, ref.shape, 1) == kv_head
        kept = jnp.sum(jnp.where(wanted, ref[...].astype(jnp.float32), 0.0), axis=1)
        kv_ref[n * span : (n + 1) * span, :] = kept.astype(kv_ref.dtype)


def allow(masks, blocks, rows, out_ref):
    heads_rows, keys = out_ref.shape
    count = blocks * rows
    span = keys // len(masks)
    n_tp = lax.axis_size("tp")
    ctx, core = lax.axis_index("ctx"), lax.axis_index("tp")
    lane = lax.broadcasted_iota(jnp.int32, (1, keys), 1)
    start = jnp.zeros_like(lane)
    for j, (even, odd) in enumerate(masks):
        block = ctx ^ jnp.where(core == 0, even, odd)
        start = jnp.where(lane // span == j, block * span, start)
    key_pos = start + lane % span
    row = lax.broadcasted_iota(jnp.int32, (heads_rows, 1), 0) % count
    query_pos = ((ctx * blocks + row // rows) * n_tp + core) * rows + row % rows
    allowed = key_pos <= query_pos
    out_ref[...] = jnp.where(allowed, 0.0, -1e30)


def route_kernel(live, blocks, masks, *refs):
    ins, (q_ref, note_ref, mix_ref, allowed_ref), held, sems = refs[:3], refs[3:7], refs[7:10], refs[10]
    copies = [pltpu.make_async_copy(i, h, sems.at[n]) for n, (i, h) in enumerate(zip(ins, held))]
    for copy in copies:
        copy.start()
    query_ref, routes_ref, weight_ref = held
    heads = query_ref.shape[1]
    mine = lax.axis_index("exp")
    allow(masks, blocks, routes_ref.shape[0], allowed_ref)
    for copy in copies:
        copy.wait()
    q_ref[...] = jnp.concatenate([query_ref[:, h, :] for h in range(heads)], axis=0)
    rows, picks = routes_ref.shape
    width = mix_ref.shape[1]
    routes, weight = routes_ref[...], weight_ref[...]
    lane = lax.broadcasted_iota(jnp.int32, (rows, width), 1)
    expert = jnp.where(lane < live * CAP, lane // CAP, -1)
    has = jnp.zeros((rows, width), jnp.float32)
    part = jnp.zeros((rows, width), jnp.float32)
    for k in range(picks):
        hit = routes[:, k : k + 1] == expert
        has = has + jnp.where(hit, 1.0, 0.0)
        part = part + jnp.where(hit, weight[:, k : k + 1], 0.0)
    earlier = [jnp.zeros((1, width), jnp.float32)]
    for r in range(rows - 1):
        earlier.append(earlier[-1] + has[r : r + 1])
    slot = jnp.concatenate(earlier, axis=0)
    hit = jnp.where(slot == (lane % CAP).astype(jnp.float32), has, 0.0)
    mix_ref[...] = hit * part / jnp.sum(weight, axis=1, keepdims=True)
    note_ref[...] = jnp.concatenate(
        [jnp.where(mine == b, hit, 0.0) for b in range(blocks)], axis=0
    ).astype(note_ref.dtype)


def attend_kernel(q_ref, allowed_ref, *refs):
    kv_refs, out_ref = refs[:-1], refs[-1]
    count = out_ref.shape[0]
    heads = q_ref.shape[0] // count
    head_dim = q_ref.shape[1]
    span = kv_refs[0].shape[0] // 2
    key = jnp.concatenate([r[:span, :] for r in kv_refs], axis=0)
    value = jnp.concatenate([r[span:, :] for r in kv_refs], axis=0)
    score = lax.dot_general(
        q_ref[...], key, (((1,), (1,)), ((), ())), preferred_element_type=jnp.float32
    ) * (head_dim ** (-0.5))
    score = score + allowed_ref[...]
    prob = jnp.exp(score - jnp.max(score, axis=1, keepdims=True))
    total = jnp.sum(prob, axis=1, keepdims=True)
    mixed = jnp.dot(prob.astype(jnp.bfloat16), value, preferred_element_type=jnp.float32) / total
    mixed = mixed.astype(jnp.bfloat16)
    for h in range(heads):
        out_ref[:, h * head_dim : (h + 1) * head_dim] = mixed[h * count : (h + 1) * count]


def turn(gate_ref, up_ref, out_ref):
    units, width = gate_ref.shape
    for at in range(0, width, LANES):
        both = jnp.concatenate([gate_ref[:, at : at + LANES], up_ref[:, at : at + LANES]], axis=0)
        out_ref[at : at + LANES, :] = both.T


def load_kernel(gate_hbm, up_hbm, down_hbm, wide_ref, down_ref, gate_ref, up_ref, sems):
    ends = ((gate_hbm, gate_ref), (up_hbm, up_ref), (down_hbm, down_ref))
    copies = [pltpu.make_async_copy(i, o, sems.at[n]) for n, (i, o) in enumerate(ends)]
    for copy in copies:
        copy.start()
    copies[0].wait()
    copies[1].wait()
    turn(gate_ref, up_ref, wide_ref)
    copies[2].wait()


def hidden_units(x, inverse, wide_ref, down_ref):
    units = down_ref.shape[0]
    both = jnp.dot(x, wide_ref[...], preferred_element_type=jnp.float32) * inverse
    hidden = silu_mul(both[:, :units], both[:, units:]).astype(jnp.bfloat16)
    return jnp.dot(hidden, down_ref[...], preferred_element_type=jnp.float32)


def experts_kernel(blocks, live, masks, parts, *refs):
    part_refs, gain_ref, refs = refs[:parts], refs[parts], refs[parts + 1 :]
    weights, own_ref, outs = refs[:4], refs[4], refs[5:]
    count, width = part_refs[0].shape[0], own_ref.shape[1]
    rows = count // blocks
    mine = lax.axis_index("exp")
    summed = sum(r[:, :width].astype(jnp.float32) for r in part_refs).astype(jnp.bfloat16)
    note = functools.reduce(lambda x, y: x + y, [r[:, width:] for r in part_refs])
    expert = lax.rem(mine, live)
    slots = blocks * CAP
    shape = (slots, note.shape[1])
    pick_lane = (
        lax.broadcasted_iota(jnp.int32, shape, 1)
        == expert * CAP + lax.broadcasted_iota(jnp.int32, shape, 0) % CAP
    )
    pick = lax.dot_general(
        pick_lane.astype(jnp.float32).astype(jnp.bfloat16),
        note,
        (((1,), (1,)), ((), ())),
        preferred_element_type=jnp.float32,
    )
    shape = (slots, count)
    place = lax.broadcasted_iota(jnp.int32, shape, 0) // CAP
    core = lax.axis_index("tp")
    mask = jnp.zeros(shape, jnp.int32)
    for i, (even, odd) in enumerate(masks):
        mask = jnp.where(place == i, jnp.where(core == 0, even, odd), mask)
    same = mask == (lax.broadcasted_iota(jnp.int32, shape, 1) // rows) ^ mine
    pick = jnp.where(same, pick, 0.0)
    shape = (rows, count)
    own = (
        lax.broadcasted_iota(jnp.int32, shape, 0) + mine * rows
        == lax.broadcasted_iota(jnp.int32, shape, 1)
    )
    pick = jnp.concatenate([pick, own.astype(jnp.float32)], axis=0).astype(jnp.bfloat16)
    picked = jnp.dot(pick, summed, preferred_element_type=jnp.float32)
    own_ref[...] = picked[slots:]
    state = picked[:slots]
    inverse = lax.rsqrt(jnp.mean(state * state, axis=1, keepdims=True) + 1e-06)
    x = (state * gain_ref[...]).astype(jnp.bfloat16)
    result = hidden_units(x, inverse, *weights[:2]) + hidden_units(x, inverse, *weights[2:])
    for m, out_ref in enumerate(outs):
        out_ref[...] = result[m * CAP : (m + 1) * CAP].astype(out_ref.dtype)


def combine_kernel(live, masks, mix_ref, own_ref, *refs):
    back_refs, (out_hbm, held_ref, sems) = refs[:-3], refs[-3:]
    mine, core = lax.axis_index("exp"), lax.axis_index("tp")
    mix = mix_ref[...]
    lane = lax.broadcasted_iota(jnp.int32, mix.shape, 1)
    shares = []
    for even, odd in masks:
        expert = lax.rem(mine ^ jnp.where(core == 0, even, odd), live)
        for s in range(CAP):
            wanted = lane == expert * CAP + s
            shares.append(jnp.sum(jnp.where(wanted, mix, 0.0), axis=1, keepdims=True))
    width = out_hbm.shape[1] // CHUNKS
    copies = []
    for n in range(CHUNKS):
        at = slice(n * width, (n + 1) * width)
        total = own_ref[:, at]
        for m, back_ref in enumerate(back_refs):
            back = back_ref[:, at].astype(jnp.float32)
            for s in range(CAP):
                total = total + shares[m * CAP + s] * back[s : s + 1]
        held_ref[:, at] = total.astype(held_ref.dtype)
        copies.append(pltpu.make_async_copy(held_ref.at[:, at], out_hbm.at[:, at], sems.at[n]))
        copies[-1].start()
    for copy in copies:
        copy.wait()


def on_device(
    queries, keys, values, out_weight, norm_gain, routes, route_weight, w_gate, w_up, w_down
):
    blocks, lanes, rows, heads, head_dim = queries.shape
    width = out_weight.shape[1]
    n_exp = lax.axis_size("exp")
    live = n_exp // 2
    count = blocks * rows
    group = heads * n_exp // keys.shape[1]
    note_width = -(-(live * CAP) // LANES) * LANES
    (kv,) = call(
        functools.partial(open_kernel, heads, group),
        [((2 * keys.shape[0], head_dim), jnp.bfloat16)],
        *far((keys, values)),
        where=pltpu.HBM,
        scratch=[pltpu.VMEM(a.shape, a.dtype) for a in (keys, values)]
        + [pltpu.SemaphoreType.DMA((2,))],
        name="open",
    )
    masks, got = gather_ctx(kv)
    weights = (w_gate[0].T, w_up[0].T, w_down[0])
    small = (queries.reshape(count, heads, head_dim), routes, route_weight)
    got[1], *tied = lax.optimization_barrier((got[1], *weights, *small))
    moved = [swap(w, "tp", 1) for w in tied[:3]]
    query, note, mix, allowed = call(
        functools.partial(route_kernel, live, blocks, masks),
        [
            ((heads * count, head_dim), jnp.bfloat16),
            ((count, note_width), jnp.bfloat16),
            ((rows, note_width), jnp.float32),
            ((heads * count, len(got) * keys.shape[0]), jnp.float32),
        ],
        *far(tied[3:]),
        where=pltpu.HBM,
        scratch=[pltpu.VMEM(a.shape, a.dtype) for a in small] + [pltpu.SemaphoreType.DMA((3,))],
        name="route",
    )
    (mixed,) = call(
        attend_kernel,
        [((count, heads * head_dim), jnp.bfloat16)],
        query,
        allowed,
        *got,
        flops=10**10,
        name="attend",
    )
    term = jnp.dot(mixed, out_weight, preferred_element_type=jnp.float32).astype(jnp.bfloat16)
    summed = jnp.concatenate([term, note], axis=1)
    units = w_down.shape[1]
    summed, *weights = lax.optimization_barrier((summed, *weights))
    weights = call(
        load_kernel,
        [((width, 2 * units), w_down.dtype), ((units, width), w_down.dtype)],
        *far(weights),
        where=pltpu.HBM,
        scratch=[pltpu.VMEM((units, width), w_down.dtype)] * 2 + [pltpu.SemaphoreType.DMA((3,))],
        read=6 * w_down.size,
        name="load",
    )
    steps = [1 << i for i in range(n_exp.bit_length() - 1)]
    for at in range(0, len(steps), 2):
        pair = steps[at : at + 2]
        low, high = pair[0], pair[-1]
        masks = [(low | high,) * 2, (low, high), (high, low)] if len(pair) == 2 else [(low, low)]
        others = [swap_by_core(summed, "exp", m) for m in masks]
        if at + 2 < len(steps):
            summed = sum(o.astype(jnp.float32) for o in others) + summed.astype(jnp.float32)
            summed = summed.astype(jnp.bfloat16)
    (wide,) = call(
        turn, [((width, 2 * units), w_down.dtype)], *moved[:2], read=4 * w_down.size, name="turn"
    )
    masks = by_distance(n_exp)
    slots = blocks * CAP
    own, *results = call(
        functools.partial(experts_kernel, blocks, live, masks, 1 + len(others)),
        [((rows, width), jnp.float32)] + [((CAP, width), jnp.bfloat16)] * n_exp,
        *others,
        summed,
        norm_gain.reshape(1, width),
        *weights,
        wide,
        moved[2],
        flops=12 * slots * w_down.size,
        read=12 * w_down.size,
        name="experts",
    )
    back = [results[0]]
    for (even, odd), result in zip(masks[1:], results[1:]):
        across = int(even.bit_count() > 1)
        result = swap_by_core(result, "exp", (even, odd), across)
        back.append(swap(result, "tp", 1) if across else result)
    (out,) = call(
        functools.partial(combine_kernel, live, masks),
        [((rows, width), jnp.bfloat16)],
        mix,
        own,
        *back,
        kept=pltpu.HBM,
        scratch=[pltpu.VMEM((rows, width), jnp.bfloat16), pltpu.SemaphoreType.DMA((CHUNKS,))],
        name="combine",
    )
    return out


def solution(mesh):
    in_specs = (
        P("ctx", "tp", None, "exp", None),
        P("ctx", None, None),
        P("ctx", None, None),
        P("exp", None),
        P(),
        P(("ctx", "exp", "tp"), None),
        P(("ctx", "exp", "tp"), None),
        P("exp", None, "tp"),
        P("exp", None, "tp"),
        P("exp", "tp", None),
    )
    out_specs = P(("ctx", "exp", "tp"), None)
    return jax.shard_map(
        on_device, mesh=mesh, in_specs=in_specs, out_specs=out_specs, check_vma=False
    )
```

```python
import functools

import jax
import jax.numpy as jnp
from jax import lax
from jax.experimental import pallas as pl
from jax.experimental.pallas import tpu as pltpu
from jax.sharding import PartitionSpec as P

CAP = 2
LANES = 128
CHUNKS = 4
VMEM_LIMIT = 24 * 1024 * 1024


def silu_mul(gate, up):
    return gate / (1.0 + jnp.exp(-gate)) * up


def swap(x, axis, mask):
    size = lax.axis_size(axis)
    return lax.ppermute(x, axis, [(i, i ^ mask) for i in range(size)])


def swap_by_core(x, axis, masks, across=0):
    size, cores = lax.axis_size(axis), lax.axis_size("tp")
    pairs = [
        (i * cores + t, (i ^ masks[t % len(masks)]) * cores + (t ^ across))
        for i in range(size)
        for t in range(cores)
    ]
    return lax.ppermute(x, (axis, "tp"), pairs)


def by_distance(size):
    far_first = sorted(range(1, size), key=lambda m: (-m.bit_count(), -m))
    return [(0, 0)] + [(m, m) for m in far_first]


def gather_ctx(x):
    size = lax.axis_size("ctx")
    masks, got = [(0, 0)], [x]
    for low in range(1, size // 2):
        high = size - low
        mine = swap_by_core(x, "ctx", (low, high))
        masks += [(low, high), (high, low)]
        got += [mine, swap(mine, "tp", 1)]
    masks.append((size // 2, size // 2))
    got.append(swap_by_core(x, "ctx", masks[-1]))
    return masks, got


def far(args):
    return [pltpu.with_memory_space_constraint(a, pltpu.HBM) for a in args]


def call(kernel, outs, *args, where=pltpu.VMEM, scratch=(), kept=pltpu.VMEM, flops=0, read=0, name=None):
    return pl.pallas_call(
        kernel,
        out_shape=[kept(shape, dtype) for shape, dtype in outs],
        in_specs=[pl.BlockSpec(memory_space=where)] * len(args),
        out_specs=[pl.BlockSpec(memory_space=pltpu.HBM if kept is pltpu.HBM else pltpu.VMEM)] * len(outs),
        scratch_shapes=scratch,
        compiler_params=pltpu.CompilerParams(vmem_limit_bytes=VMEM_LIMIT),
        cost_estimate=pl.CostEstimate(flops=flops, bytes_accessed=read, transcendentals=0),
        name=name,
    )(*args)


def open_kernel(heads, group, key_hbm, value_hbm, kv_ref, key_ref, value_ref, sems):
    copies = [
        pltpu.make_async_copy(key_hbm, key_ref, sems.at[0]),
        pltpu.make_async_copy(value_hbm, value_ref, sems.at[1]),
    ]
    for copy in copies:
        copy.start()
    span = key_ref.shape[0]
    kv_head = lax.axis_index("exp") * heads // group
    for n, ref in enumerate((key_ref, value_ref)):
        copies[n].wait()
        wanted = lax.broadcasted_iota(jnp.int32, ref.shape, 1) == kv_head
        kept = jnp.sum(jnp.where(wanted, ref[...].astype(jnp.float32), 0.0), axis=1)
        kv_ref[n * span : (n + 1) * span, :] = kept.astype(kv_ref.dtype)


def allow(masks, blocks, rows, out_ref):
    heads_rows, keys = out_ref.shape
    count = blocks * rows
    span = keys // len(masks)
    n_tp = lax.axis_size("tp")
    ctx, core = lax.axis_index("ctx"), lax.axis_index("tp")
    lane = lax.broadcasted_iota(jnp.int32, (1, keys), 1)
    start = jnp.zeros_like(lane)
    for j, (even, odd) in enumerate(masks):
        block = ctx ^ jnp.where(core == 0, even, odd)
        start = jnp.where(lane // span == j, block * span, start)
    key_pos = start + lane % span
    row = lax.broadcasted_iota(jnp.int32, (heads_rows, 1), 0) % count
    query_pos = ((ctx * blocks + row // rows) * n_tp + core) * rows + row % rows
    allowed = key_pos <= query_pos
    out_ref[...] = jnp.where(allowed, 0.0, -1e30)


def route_kernel(live, blocks, masks, *refs):
    ins, (q_ref, note_ref, mix_ref, allowed_ref), held, sems = refs[:3], refs[3:7], refs[7:10], refs[10]
    copies = [pltpu.make_async_copy(i, h, sems.at[n]) for n, (i, h) in enumerate(zip(ins, held))]
    for copy in copies:
        copy.start()
    query_ref, routes_ref, weight_ref = held
    heads = query_ref.shape[1]
    mine = lax.axis_index("exp")
    allow(masks, blocks, routes_ref.shape[0], allowed_ref)
    for copy in copies:
        copy.wait()
    q_ref[...] = jnp.concatenate([query_ref[:, h, :] for h in range(heads)], axis=0)
    rows, picks = routes_ref.shape
    width = mix_ref.shape[1]
    routes, weight = routes_ref[...], weight_ref[...]
    lane = lax.broadcasted_iota(jnp.int32, (rows, width), 1)
    expert = jnp.where(lane < live * CAP, lane // CAP, -1)
    has = jnp.zeros((rows, width), jnp.float32)
    part = jnp.zeros((rows, width), jnp.float32)
    for k in range(picks):
        hit = routes[:, k : k + 1] == expert
        has = has + jnp.where(hit, 1.0, 0.0)
        part = part + jnp.where(hit, weight[:, k : k + 1], 0.0)
    earlier = [jnp.zeros((1, width), jnp.float32)]
    for r in range(rows - 1):
        earlier.append(earlier[-1] + has[r : r + 1])
    slot = jnp.concatenate(earlier, axis=0)
    hit = jnp.where(slot == (lane % CAP).astype(jnp.float32), has, 0.0)
    mix_ref[...] = hit * part / jnp.sum(weight, axis=1, keepdims=True)
    note_ref[...] = jnp.concatenate(
        [jnp.where(mine == b, hit, 0.0) for b in range(blocks)], axis=0
    ).astype(note_ref.dtype)


def attend_kernel(q_ref, allowed_ref, *refs):
    kv_refs, out_ref = refs[:-1], refs[-1]
    count = out_ref.shape[0]
    heads = q_ref.shape[0] // count
    head_dim = q_ref.shape[1]
    span = kv_refs[0].shape[0] // 2
    key = jnp.concatenate([r[:span, :] for r in kv_refs], axis=0)
    value = jnp.concatenate([r[span:, :] for r in kv_refs], axis=0)
    score = lax.dot_general(
        q_ref[...], key, (((1,), (1,)), ((), ())), preferred_element_type=jnp.float32
    ) * (head_dim ** (-0.5))
    score = score + allowed_ref[...]
    prob = jnp.exp(score - jnp.max(score, axis=1, keepdims=True))
    total = jnp.sum(prob, axis=1, keepdims=True)
    mixed = jnp.dot(prob.astype(jnp.bfloat16), value, preferred_element_type=jnp.float32) / total
    mixed = mixed.astype(jnp.bfloat16)
    for h in range(heads):
        out_ref[:, h * head_dim : (h + 1) * head_dim] = mixed[h * count : (h + 1) * count]


def turn(gate_ref, up_ref, out_ref):
    units, width = gate_ref.shape
    for at in range(0, width, LANES):
        both = jnp.concatenate([gate_ref[:, at : at + LANES], up_ref[:, at : at + LANES]], axis=0)
        out_ref[at : at + LANES, :] = both.T


def load_kernel(gate_hbm, up_hbm, down_hbm, wide_ref, down_ref, gate_ref, up_ref, sems):
    ends = ((gate_hbm, gate_ref), (up_hbm, up_ref), (down_hbm, down_ref))
    copies = [pltpu.make_async_copy(i, o, sems.at[n]) for n, (i, o) in enumerate(ends)]
    for copy in copies:
        copy.start()
    copies[0].wait()
    copies[1].wait()
    turn(gate_ref, up_ref, wide_ref)
    copies[2].wait()


def hidden_units(x, inverse, wide_ref, down_ref):
    units = down_ref.shape[0]
    both = jnp.dot(x, wide_ref[...], preferred_element_type=jnp.float32) * inverse
    hidden = silu_mul(both[:, :units], both[:, units:]).astype(jnp.bfloat16)
    return jnp.dot(hidden, down_ref[...], preferred_element_type=jnp.float32)


def experts_kernel(blocks, live, masks, parts, *refs):
    part_refs, gain_ref, refs = refs[:parts], refs[parts], refs[parts + 1 :]
    weights, own_ref, outs = refs[:4], refs[4], refs[5:]
    count, width = part_refs[0].shape[0], own_ref.shape[1]
    rows = count // blocks
    mine = lax.axis_index("exp")
    summed = sum(r[:, :width].astype(jnp.float32) for r in part_refs).astype(jnp.bfloat16)
    note = functools.reduce(lambda x, y: x + y, [r[:, width:] for r in part_refs])
    expert = lax.rem(mine, live)
    slots = blocks * CAP
    shape = (slots, note.shape[1])
    pick_lane = (
        lax.broadcasted_iota(jnp.int32, shape, 1)
        == expert * CAP + lax.broadcasted_iota(jnp.int32, shape, 0) % CAP
    )
    pick = lax.dot_general(
        pick_lane.astype(jnp.float32).astype(jnp.bfloat16),
        note,
        (((1,), (1,)), ((), ())),
        preferred_element_type=jnp.float32,
    )
    shape = (slots, count)
    place = lax.broadcasted_iota(jnp.int32, shape, 0) // CAP
    core = lax.axis_index("tp")
    mask = jnp.zeros(shape, jnp.int32)
    for i, (even, odd) in enumerate(masks):
        mask = jnp.where(place == i, jnp.where(core == 0, even, odd), mask)
    same = mask == (lax.broadcasted_iota(jnp.int32, shape, 1) // rows) ^ mine
    pick = jnp.where(same, pick, 0.0)
    shape = (rows, count)
    own = (
        lax.broadcasted_iota(jnp.int32, shape, 0) + mine * rows
        == lax.broadcasted_iota(jnp.int32, shape, 1)
    )
    pick = jnp.concatenate([pick, own.astype(jnp.float32)], axis=0).astype(jnp.bfloat16)
    picked = jnp.dot(pick, summed, preferred_element_type=jnp.float32)
    own_ref[...] = picked[slots:]
    state = picked[:slots]
    inverse = lax.rsqrt(jnp.mean(state * state, axis=1, keepdims=True) + 1e-06)
    x = (state * gain_ref[...]).astype(jnp.bfloat16)
    result = hidden_units(x, inverse, *weights[:2]) + hidden_units(x, inverse, *weights[2:])
    for m, out_ref in enumerate(outs):
        out_ref[...] = result[m * CAP : (m + 1) * CAP].astype(out_ref.dtype)


def combine_kernel(live, masks, mix_ref, own_ref, *refs):
    back_refs, (out_hbm, held_ref, sems) = refs[:-3], refs[-3:]
    mine, core = lax.axis_index("exp"), lax.axis_index("tp")
    mix = mix_ref[...]
    lane = lax.broadcasted_iota(jnp.int32, mix.shape, 1)
    shares = []
    for even, odd in masks:
        expert = lax.rem(mine ^ jnp.where(core == 0, even, odd), live)
        for s in range(CAP):
            wanted = lane == expert * CAP + s
            shares.append(jnp.sum(jnp.where(wanted, mix, 0.0), axis=1, keepdims=True))
    width = out_hbm.shape[1] // CHUNKS
    copies = []
    for n in range(CHUNKS):
        at = slice(n * width, (n + 1) * width)
        total = own_ref[:, at]
        for m, back_ref in enumerate(back_refs):
            back = back_ref[:, at].astype(jnp.float32)
            for s in range(CAP):
                total = total + shares[m * CAP + s] * back[s : s + 1]
        held_ref[:, at] = total.astype(held_ref.dtype)
        copies.append(pltpu.make_async_copy(held_ref.at[:, at], out_hbm.at[:, at], sems.at[n]))
        copies[-1].start()
    for copy in copies:
        copy.wait()


def on_device(
    queries, keys, values, out_weight, norm_gain, routes, route_weight, w_gate, w_up, w_down
):
    blocks, lanes, rows, heads, head_dim = queries.shape
    width = out_weight.shape[1]
    n_exp = lax.axis_size("exp")
    live = n_exp // 2
    count = blocks * rows
    group = heads * n_exp // keys.shape[1]
    note_width = -(-(live * CAP) // LANES) * LANES
    (kv,) = call(
        functools.partial(open_kernel, heads, group),
        [((2 * keys.shape[0], head_dim), jnp.bfloat16)],
        *far((keys, values)),
        where=pltpu.HBM,
        scratch=[pltpu.VMEM(a.shape, a.dtype) for a in (keys, values)]
        + [pltpu.SemaphoreType.DMA((2,))],
        name="open",
    )
    masks, got = gather_ctx(kv)
    weights = (w_gate[0].T, w_up[0].T, w_down[0])
    small = (queries.reshape(count, heads, head_dim), routes, route_weight)
    got[1], *tied = lax.optimization_barrier((got[1], *weights, *small))
    moved = [swap(w, "tp", 1) for w in tied[:3]]
    query, note, mix, allowed = call(
        functools.partial(route_kernel, live, blocks, masks),
        [
            ((heads * count, head_dim), jnp.bfloat16),
            ((count, note_width), jnp.bfloat16),
            ((rows, note_width), jnp.float32),
            ((heads * count, len(got) * keys.shape[0]), jnp.float32),
        ],
        *far(tied[3:]),
        where=pltpu.HBM,
        scratch=[pltpu.VMEM(a.shape, a.dtype) for a in small] + [pltpu.SemaphoreType.DMA((3,))],
        name="route",
    )
    (mixed,) = call(
        attend_kernel,
        [((count, heads * head_dim), jnp.bfloat16)],
        query,
        allowed,
        *got,
        flops=10**10,
        name="attend",
    )
    term = jnp.dot(mixed, out_weight, preferred_element_type=jnp.float32).astype(jnp.bfloat16)
    summed = jnp.concatenate([term, note], axis=1)
    units = w_down.shape[1]
    summed, *weights = lax.optimization_barrier((summed, *weights))
    weights = call(
        load_kernel,
        [((width, 2 * units), w_down.dtype), ((units, width), w_down.dtype)],
        *far(weights),
        where=pltpu.HBM,
        scratch=[pltpu.VMEM((units, width), w_down.dtype)] * 2 + [pltpu.SemaphoreType.DMA((3,))],
        read=6 * w_down.size,
        name="load",
    )
    steps = [1 << i for i in range(n_exp.bit_length() - 1)]
    for at in range(0, len(steps), 2):
        pair = steps[at : at + 2]
        low, high = pair[0], pair[-1]
        masks = [(low | high,) * 2, (low, high), (high, low)] if len(pair) == 2 else [(low, low)]
        others = [swap_by_core(summed, "exp", m) for m in masks]
        if at + 2 < len(steps):
            summed = sum(o.astype(jnp.float32) for o in others) + summed.astype(jnp.float32)
            summed = summed.astype(jnp.bfloat16)
    (wide,) = call(
        turn, [((width, 2 * units), w_down.dtype)], *moved[:2], read=4 * w_down.size, name="turn"
    )
    masks = by_distance(n_exp)
    slots = blocks * CAP
    own, *results = call(
        functools.partial(experts_kernel, blocks, live, masks, 1 + len(others)),
        [((rows, width), jnp.float32)] + [((CAP, width), jnp.bfloat16)] * n_exp,
        *others,
        summed,
        norm_gain.reshape(1, width),
        *weights,
        wide,
        moved[2],
        flops=12 * slots * w_down.size,
        read=12 * w_down.size,
        name="experts",
    )
    back = [results[0]]
    for (even, odd), result in zip(masks[1:], results[1:]):
        across = int(even.bit_count() > 1)
        result = swap_by_core(result, "exp", (even, odd), across)
        back.append(swap(result, "tp", 1) if across else result)
    (out,) = call(
        functools.partial(combine_kernel, live, masks),
        [((rows, width), jnp.bfloat16)],
        mix,
        own,
        *back,
        kept=pltpu.HBM,
        scratch=[pltpu.VMEM((rows, width), jnp.bfloat16), pltpu.SemaphoreType.DMA((CHUNKS,))],
        name="combine",
    )
    return out


def solution(mesh):
    in_specs = (
        P("ctx", "tp", None, "exp", None),
        P("ctx", None, None),
        P("ctx", None, None),
        P("exp", None),
        P(),
        P(("ctx", "exp", "tp"), None),
        P(("ctx", "exp", "tp"), None),
        P("exp", None, "tp"),
        P("exp", None, "tp"),
        P("exp", "tp", None),
    )
    out_specs = P(("ctx", "exp", "tp"), None)
    return jax.shard_map(
        on_device, mesh=mesh, in_specs=in_specs, out_specs=out_specs, check_vma=False
    )
```
